512 devices in a mesh: sx: 4 (over y_lo, core), sy: 8 (over z), af: 16 (over y_hi, x).
Axes of the slice: x: 4, y: 8 (y_hi: 4, y_lo: 2; y = y_hi * 2 + y_lo), z: 8, core: 2. Of those that a mesh axis runs over, the one named last changes fastest.
Arguments:
- inputs: bfloat16 [32, 32, 8, 4, 512], P(None, 'af', 'sy', 'sx'), may hold values from -6 to 6
- weight_one: bfloat16 [27, 64, 32], replicated, may hold values from -0.21875 to 0.21875
- weight_two: bfloat16 [27, 128, 64], P(None, 'af'), may hold values from -0.15625 to 0.15625
- cotangent: bfloat16 [128, 16, 8, 4, 128], P(None, 'af', 'sy', 'sx'), may hold values from -6 to 6
Outputs:
- output: bfloat16 [128, 16, 8, 4, 128], P(None, 'af', 'sy', 'sx')
- grad_one: float32 [27, 64, 32], replicated
- grad_two: float32 [27, 128, 64], P(None, 'af')
The draws below stay inside these ranges and needn't reach their ends.
All inputs are finite; a program needn't handle non-finite values.
Results may differ from the reference program's by a relative error of at most 0.02.
The reference program's roundings to bfloat16 on the way count: a program that leaves them out, or rounds other values in their place, can miss the bound.
Values may be sent and summed in bfloat16 or wider, within the bound.
A program may use at most 64 MiB of HBM per device.

```python
import jax
import jax.numpy as jnp
from jax import lax

CI = 32
CM = 64
CO = 128
BX = 32
BY = 16
NX = 128
NY = 128
NZ = 32
N_SX = 4
N_SY = 8


def shard_levels(key, extent, shards, least, high):
    factor_of, own = 1.0, jax.random.fold_in(key, 6)
    for dim, blocks in shards:
        heights = jnp.exp(jax.random.uniform(jax.random.fold_in(own, dim), (blocks,), jnp.float32, least / len(shards), high / len(shards)))
        factor_of = factor_of * jnp.repeat(heights, extent[dim] // blocks).reshape([-1 if axis == dim else 1 for axis in range(len(extent))])
    return factor_of


def scatter_about(key, extent, width, bound, cuts=(), dtype=jnp.bfloat16):
    gain = shard_levels(key, extent, cuts, -0.22, 0.18) if cuts else 1.0
    drawn = jax.random.normal(key, extent, jnp.float32) * width * gain
    return jnp.minimum(jnp.maximum(drawn, -bound), bound).astype(dtype)


def setup_inputs(seed: int = 0) -> dict:
    splits = jax.random.split(jax.random.key(seed), 5)
    return {
        "inputs": scatter_about(splits[0], (CI, NZ, N_SY, N_SX, BY * BX), 1.0, 6.0, ((1, 16), (2, 8), (3, 4))),
        "weight_one": scatter_about(splits[1], (27, CM, CI), (27 * CI) ** -0.5, 0.21875),
        "weight_two": scatter_about(splits[2], (27, CO, CM), (27 * CM) ** -0.5, 0.15625, ((1, 16),)),
        "cotangent": scatter_about(splits[3], (CO, NZ // 2, N_SY, N_SX, BY * BX // 4), 1.0, 6.0, ((1, 16), (2, 8), (3, 4))),
    }


def leaky(values):
    return jnp.where(values > 0, values, 0.3 * values)

def slope(values):
    return jnp.where(values > 0, 1.0, 0.3)

def from_blocks(blocks, height, breadth):
    channels, planes, rows_blk, cols_blk, _ = blocks.shape
    split = blocks.reshape(channels, planes, rows_blk, cols_blk, height, breadth)
    return split.transpose(0, 1, 2, 4, 3, 5).reshape(channels, planes, rows_blk * height, cols_blk * breadth)

def to_blocks(field, rows_blk, cols_blk):
    channels, planes, total_h, total_w = field.shape
    height = total_h // rows_blk
    breadth = total_w // cols_blk
    split = field.reshape(channels, planes, rows_blk, height, cols_blk, breadth)
    return split.transpose(0, 1, 2, 4, 3, 5).reshape(channels, planes, rows_blk, cols_blk, height * breadth)

def convolve(field, weight):
    outputs = weight.shape[1]
    channels = weight.shape[2]
    kernel = weight.reshape(3, 3, 3, outputs, channels).transpose(3, 4, 0, 1, 2)
    result = lax.conv_general_dilated(field[None], kernel, (1, 1, 1), 'SAME', dimension_numbers=('NCDHW', 'OIDHW', 'NCDHW'), preferred_element_type=jnp.float32)
    return result[0]

def flip_weight(weight):
    outputs = weight.shape[1]
    channels = weight.shape[2]
    flipped = weight.reshape(3, 3, 3, outputs, channels)[::-1, ::-1, ::-1]
    return flipped.reshape(27, outputs, channels).transpose(0, 2, 1)

def pool(values):
    channels, planes, height, breadth = values.shape
    cubes = values.reshape(channels, planes // 2, 2, height // 2, 2, breadth // 2, 2)
    return lax.optimization_barrier(jnp.sum(cubes, axis=(2, 4, 6))) * 0.125

def upsample(values):
    channels, planes, height, breadth = values.shape
    spread = jnp.broadcast_to(values[:, :, None, :, None, :, None], (channels, planes, 2, height, 2, breadth, 2))
    return spread.reshape(channels, planes * 2, height * 2, breadth * 2)

def weight_grad(field, delta):
    channels, planes, height, breadth = field.shape
    padded = jnp.pad(field, ((0, 0), (1, 1), (1, 1), (1, 1)))
    flat_delta = delta.reshape(delta.shape[0], -1)
    terms = []
    for position in range(27):
        first, second, third = (position // 9, position // 3 % 3, position % 3)
        shifted = padded[:, first:first + planes, second:second + height, third:third + breadth].reshape(channels, -1)
        terms.append(jnp.dot(flat_delta, shifted.T, preferred_element_type=jnp.float32))
    return jnp.stack(terms, 0)

def reference(inputs, weight_one, weight_two, cotangent):
    cell_count = NX * NY * NZ
    field_in = from_blocks(inputs, BY, BX)
    upstream = from_blocks(cotangent, BY // 2, BX // 2)
    hidden_one = convolve(field_in, weight_one)
    pooled = pool(leaky(hidden_one)).astype(jnp.bfloat16)
    hidden_two = convolve(pooled, weight_two)
    output = to_blocks(leaky(hidden_two).astype(jnp.bfloat16), N_SY, N_SX)
    delta_two = (upstream.astype(jnp.float32) * slope(hidden_two)).astype(jnp.bfloat16)
    grad_two = weight_grad(pooled, delta_two) * (cell_count / 8.0) ** (-0.5)
    pooled_grad = convolve(delta_two, flip_weight(weight_two)).astype(jnp.bfloat16)
    delta_one = (upsample(pooled_grad.astype(jnp.float32) * 0.125) * slope(hidden_one)).astype(jnp.bfloat16)
    grad_one = weight_grad(field_in, delta_one) * (cell_count * 1.0) ** (-0.5)
    return (output, grad_one, grad_two)
```

```python
import functools

import jax
import jax.numpy as jnp
from jax import lax
from jax.experimental import pallas as pl
from jax.experimental.pallas import tpu as pltpu
from jax.sharding import PartitionSpec as P

MESH = pl.DeviceIdType.MESH
BF16 = jnp.bfloat16
F32 = jnp.float32
N_SX, N_SY, N_AF = 4, 8, 16
SLOTS = [(dx, dy) for dy in (-1, 0, 1) for dx in (-1, 0, 1) if (dx, dy) != (0, 0)]


def iota(shape, axis):
    return lax.broadcasted_iota(jnp.int32, shape, axis)


def leaky(values):
    return jnp.where(values > 0, values, 0.3 * values)


def slope(values):
    return jnp.where(values > 0, 1.0, 0.3)


def one_hot(rows, source):
    return (iota((rows, source.shape[1]), 0) == source).astype(F32).astype(BF16)


def dot(a, b):
    return jnp.dot(a, b, preferred_element_type=F32)


def dot_nt(a, b):
    return lax.dot_general(a, b, (((1,), (1,)), ((), ())), preferred_element_type=F32)


def rolled(values, shift):
    shift = shift % values.shape[1]
    return values if shift == 0 else pltpu.roll(values, shift, 1)


def border_selection_one():
    lane = iota((1, 128), 1)
    source = jnp.full((1, 128), -1, jnp.int32)
    source = jnp.where(lane == 0, 511, source)
    source = jnp.where((lane >= 1) & (lane <= 16), 32 * (lane - 1) + 31, source)
    source = jnp.where(lane == 17, 31, source)
    source = jnp.where((lane >= 32) & (lane < 64), 480 + lane - 32, source)
    source = jnp.where(lane == 64, 480, source)
    source = jnp.where((lane >= 65) & (lane <= 80), 32 * (lane - 65), source)
    source = jnp.where(lane == 81, 0, source)
    source = jnp.where(lane >= 96, lane - 96, source)
    return one_hot(512, source)


def column_placement_one():
    lane = iota((1, 1536), 1)
    offset = lane // 512
    y = lane % 512 // 32
    x = lane % 32
    source = jnp.where(x == 0, y + offset, jnp.where(x == 31, 64 + y + offset, -1))
    return one_hot(128, source)


def border_selection_two():
    lane = iota((1, 256), 1)
    plane = lane % 128 // 32
    r = lane % 32
    rows = jnp.where(r < 16, 112 + r, r - 16)
    columns = jnp.full((1, 256), -1000, jnp.int32)
    columns = jnp.where(r == 0, 127, columns)
    columns = jnp.where((r >= 1) & (r <= 8), 16 * (r - 1) + 15, columns)
    columns = jnp.where(r == 9, 15, columns)
    columns = jnp.where(r == 16, 112, columns)
    columns = jnp.where((r >= 17) & (r <= 24), 16 * (r - 17), columns)
    columns = jnp.where(r == 25, 0, columns)
    source = 128 * plane + jnp.where(lane < 128, rows, columns)
    return one_hot(384, jnp.where(plane < 3, source, -1))


def column_placement_two():
    lane = iota((1, 1152), 1)
    plane = lane // 384
    offset = lane // 128 % 3
    y = lane % 128 // 16
    x = lane % 16
    source = jnp.where(x == 0, y + offset, jnp.where(x == 15, 16 + y + offset, -1000))
    return one_hot(128, 32 * plane + source)


def pool_selection():
    lane = iota((1, 128), 1)
    return one_hot(512, 64 * (lane // 16) + 2 * (lane % 16))


def spread_selection():
    lane = iota((1, 512), 1)
    return one_hot(128, 16 * (lane // 64) + lane % 32 // 2)


def kernel(
    x_ref, w1_ref, w2_ref, cot_ref,
    out_ref, grad_one_ref, grad_two_ref,
    x_all, w1_cat, w2_all, pack_one, recv_one, patches_one, hidden_one,
    p_all, pack_p, recv_p, patches_two,
    d_all, pack_d, recv_d, w2_turned, patches_d,
    g2_send, g2_recv, g2_tiles, g2_sy, g2_sx, g2_done,
    g1_full, g1_send, g1_sx, g1_tiles, g1_sy, g1_af, g1_part, g1_done,
    z_sems, plane_sems, w2_sems, g2_sems, g2_sy_sems, g2_sx_sems, g2_done_sems,
    g1_sx_sems, g1_sy_sems, g1_af_sems, g1_part_sems, g1_done_sems,
):
    sx, sy, af = lax.axis_index("sx"), lax.axis_index("sy"), lax.axis_index("af")

    barrier = pltpu.get_barrier_semaphore()
    for axis, me, count in (("sx", sx, N_SX), ("sy", sy, N_SY), ("af", af, N_AF)):

        def greet(j, carry, axis=axis, me=me, count=count):
            pl.semaphore_signal(
                barrier, inc=1, device_id={axis: lax.rem(me + j, count)}, device_id_type=MESH
            )
            return carry

        lax.fori_loop(1, count, greet, 0)
    for dx in (1, N_SX - 1):
        for dy in (1, N_SY - 1):
            pl.semaphore_signal(
                barrier,
                inc=1,
                device_id={"sx": lax.rem(sx + dx, N_SX), "sy": lax.rem(sy + dy, N_SY)},
                device_id_type=MESH,
            )
    pl.semaphore_wait(barrier, N_SX + N_SY + N_AF + 1)

    pending = []

    class Ring:
        def __init__(self, axis, me, count, source, target, sems):
            self.count = count

            def copy(j):
                peer = lax.rem(me + j, count)
                return pltpu.make_async_remote_copy(
                    src_ref=source(peer),
                    dst_ref=target.at[me],
                    send_sem=sems.at[0, j],
                    recv_sem=sems.at[1, j],
                    device_id={axis: peer},
                    device_id_type=MESH,
                )

            self.copy = copy
            self.each(lambda copy: copy.start())
            pending.append(self.wait_send)

        def each(self, act):
            def body(j, carry):
                act(self.copy(j))
                return carry

            lax.fori_loop(1, self.count, body, 0)

        def wait_recv(self):
            self.each(lambda copy: copy.wait_recv())

        def wait_send(self):
            self.each(lambda copy: copy.wait_send())

    def exchange_planes(low, high, target, index):
        last = target.shape[0] - 1
        copies = [
            pltpu.make_async_remote_copy(
                src_ref=source,
                dst_ref=target.at[slot],
                send_sem=z_sems.at[0, index, way],
                recv_sem=z_sems.at[1, index, way],
                device_id={"af": lax.rem(af + step, N_AF)},
                device_id_type=MESH,
            )
            for way, (source, slot, step) in enumerate(((low, last, N_AF - 1), (high, 0, 1)))
        ]
        for copy in copies:
            copy.start()
            pending.append(copy.wait_send)
        return copies

    def exchange_borders(source, target, index):
        copies = []
        for slot, (dx, dy) in enumerate(SLOTS):
            copy = pltpu.make_async_remote_copy(
                src_ref=source(dx, dy),
                dst_ref=target.at[slot],
                send_sem=plane_sems.at[0, index, slot],
                recv_sem=plane_sems.at[1, index, slot],
                device_id={
                    "sx": lax.rem(sx + N_SX - dx, N_SX),
                    "sy": lax.rem(sy + N_SY - dy, N_SY),
                },
                device_id_type=MESH,
            )
            copy.start()
            pending.append(copy.wait_send)
            copies.append(copy)
        return copies

    def inside(dx, dy):
        good = True
        if dx:
            good = (sx > 0) if dx < 0 else (sx < N_SX - 1)
        if dy:
            row = (sy > 0) if dy < 0 else (sy < N_SY - 1)
            good = row if good is True else good & row
        return good

    def gather_columns(received, height, right):
        first = received[0].astype(F32)
        lane = iota(first.shape, 1)
        r = lane if right == 64 else lane % 32
        columns = jnp.zeros(first.shape, F32)
        for dx, start in ((-1, 0), (1, right)):
            for dy, cells in (
                (0, (r >= start + 1) & (r <= start + height)),
                (-1, r == start),
                (1, r == start + height + 1),
            ):
                values = received[SLOTS.index((dx, dy))].astype(F32)
                columns = jnp.where(cells & inside(dx, dy), values, columns)
        return columns.astype(BF16)

    def masked_rows(received, dy):
        values = received[SLOTS.index((0, dy))].astype(F32)
        return jnp.where(inside(0, dy), values, 0.0)

    x_copies = exchange_planes(x_ref.at[0], x_ref.at[1], x_all, 0)
    w2_ring = Ring("af", af, N_AF, lambda peer: w2_ref, w2_all, w2_sems)
    w2_all[af] = w2_ref[...]
    x_all[1] = x_ref[0]
    x_all[2] = x_ref[1]
    for k in range(27):
        w1_cat[:, 32 * k : 32 * k + 32] = w1_ref[k]
    selection = border_selection_one()
    for copy in x_copies:
        copy.wait_recv()

    field = x_all[...].reshape(128, 512).astype(F32)
    row = iota((128, 512), 0)
    outer = ((row < 32) & (af == 0)) | ((row >= 96) & (af == N_AF - 1))
    field = jnp.where(outer, 0.0, field)
    pack_one[...] = dot(field.astype(BF16), selection).astype(BF16)
    copies = exchange_borders(lambda dx, dy: pack_one, recv_one, 0)
    placement = column_placement_one()
    for copy in copies:
        copy.wait_recv()
    columns = dot(gather_columns(recv_one, 16, 64), placement)
    above, below = masked_rows(recv_one, -1), masked_rows(recv_one, 1)
    lane = iota((128, 128), 1)
    x = iota((128, 512), 1) % 32
    for b in range(3):
        for c in range(3):
            dy, dx = b - 1, c - 1
            moved = rolled(field, -(32 * dy + dx))
            if dy == -1:
                first = jnp.where(lane < 32, rolled(above, -(32 + dx)), moved[:, :128])
                moved = jnp.concatenate([first, moved[:, 128:]], axis=1)
            if dy == 1:
                final = jnp.where(lane >= 96, rolled(below, -dx), moved[:, 384:])
                moved = jnp.concatenate([moved[:, :384], final], axis=1)
            if dx:
                placed = columns[:, 512 * b : 512 * b + 512]
                moved = jnp.where(x == (0 if dx < 0 else 31), placed, moved)
            moved = moved.astype(BF16)
            start = 32 * (3 * b + c)
            for z in range(4):
                patches_one[288 * z + start : 288 * z + start + 32] = moved[32 * z : 32 * z + 32]
    total = None
    for z in range(2):
        hidden = dot(w1_cat[...], patches_one[288 * z : 288 * z + 864])
        hidden_one[z] = hidden
        total = leaky(hidden) if total is None else total + leaky(hidden)
    total = total + rolled(total, -1)
    total = total + rolled(total, -32)
    pooled = dot((total * 0.125).astype(BF16), pool_selection()).astype(BF16)

    def second_shifts(field_all, pack, received, index, visit):
        channels = field_all.shape[1]
        planes = []
        for z in range(3):
            values = field_all[z].astype(F32)
            if z != 1:
                values = jnp.where(af > 0 if z == 0 else af < N_AF - 1, values, 0.0)
            planes.append(values)
        joined = jnp.concatenate([values.astype(BF16) for values in planes], axis=1)
        packed = dot(joined, border_selection_two()).astype(BF16)
        pack[0] = packed[:, :128]
        pack[1] = packed[:, 128:]
        copies = exchange_borders(lambda dx, dy: pack.at[0 if dx == 0 else 1], received, index)
        placement = column_placement_two()
        for copy in copies:
            copy.wait_recv()
        columns = dot(gather_columns(received, 8, 16), placement)
        above, below = masked_rows(received, -1), masked_rows(received, 1)
        lane = iota((channels, 128), 1)
        x = lane % 16
        for k in range(27):
            z, dy, dx = k // 9, k // 3 % 3 - 1, k % 3 - 1
            moved = rolled(planes[z], -(16 * dy + dx))
            if dy == -1:
                moved = jnp.where(lane < 16, rolled(above, -(32 * z + dx)), moved)
            if dy == 1:
                moved = jnp.where(lane >= 112, rolled(below, 96 - 32 * z - dx), moved)
            if dx:
                place = 128 * (k // 3)
                moved = jnp.where(
                    x == (0 if dx < 0 else 15), columns[:, place : place + 128], moved
                )
            visit(k, moved)

    p_all[1] = pooled
    copies = exchange_planes(p_all.at[1], p_all.at[1], p_all, 1)
    for copy in copies:
        copy.wait_recv()

    def keep_pooled(k, values):
        half, place = k // 14, k % 14
        patches_two[64 * place : 64 * place + 64, 128 * half : 128 * half + 128] = values.astype(BF16)

    patches_two[832:896, 128:256] = jnp.zeros((64, 128), BF16)
    second_shifts(p_all, pack_p, recv_p, 1, keep_pooled)
    w2_ring.wait_recv()
    filters = w2_all[...].reshape(256, 896)
    product = dot(filters, patches_two[...]).reshape(16, 2, 8, 256)
    hidden_two = (product[:, 0, :, :128] + product[:, 1, :, 128:]).reshape(128, 128)
    out_ref[...] = leaky(hidden_two).astype(BF16)
    delta_two = (cot_ref[...].astype(F32) * slope(hidden_two)).astype(BF16)
    d_all[1] = delta_two
    copies = exchange_planes(d_all.at[1], d_all.at[1], d_all, 2)

    halves = [
        dot_nt(delta_two, patches_two[:, 128 * half : 128 * half + 128]).reshape(16, 1, 8, 896)
        for half in range(2)
    ]
    g2_send[...] = jnp.concatenate(halves, axis=1).reshape(16, 16, 896).astype(BF16)
    turned = filters.astype(F32).T.astype(BF16)
    for place in range(14):
        w2_turned[:, 256 * place : 256 * place + 256] = turned[64 * place : 64 * place + 64]
    for copy in copies:
        copy.wait_recv()
    held = {}

    def keep_delta(k, values):
        held[26 - k] = values.reshape(16, 1, 8, 128)

    second_shifts(d_all, pack_d, recv_d, 2, keep_delta)
    g2_ring = Ring("af", af, N_AF, lambda peer: g2_send.at[peer], g2_recv, g2_sems)
    g2_recv[af] = g2_send[af]
    held[27] = jnp.zeros((16, 1, 8, 128), F32)
    for place in range(14):
        both = jnp.concatenate([held[place], held[place + 14]], axis=1)
        patches_d[256 * place : 256 * place + 256] = both.reshape(256, 128).astype(BF16)
    pooled_grad = dot(w2_turned[...], patches_d[...]).astype(BF16)

    spread = dot(pooled_grad, spread_selection()) * 0.125
    total = None
    for z in range(2):
        delta_one = (spread * slope(hidden_one[z])).astype(BF16)
        part = dot_nt(delta_one, patches_one[288 * z : 288 * z + 864])
        total = part if total is None else total + part
    g1_full[...] = jnp.zeros((64, 896), F32)
    g1_full[:, :864] = total
    g1_send[...] = g1_full[...].astype(BF16).reshape(4, 16, 896)
    g1_sx_ring = Ring("sx", sx, N_SX, lambda peer: g1_send.at[peer], g1_sx, g1_sx_sems)
    g1_sx[sx] = g1_send[sx]

    def to_tiles(values, tiles):
        for t in range(7):
            tiles[t] = values[:, 128 * t : 128 * t + 128]
        tiles[7] = jnp.zeros((16, 128), F32)

    g2_ring.wait_recv()
    to_tiles(jnp.sum(g2_recv[...].astype(F32), axis=0), g2_tiles)
    g2_sy_ring = Ring("sy", sy, N_SY, lambda peer: g2_tiles.at[peer], g2_sy, g2_sy_sems)
    g2_sy[sy] = g2_tiles[sy]

    g1_sx_ring.wait_recv()
    to_tiles(jnp.sum(g1_sx[...].astype(F32), axis=0), g1_tiles)
    g1_sy_ring = Ring("sy", sy, N_SY, lambda peer: g1_tiles.at[peer], g1_sy, g1_sy_sems)
    g1_sy[sy] = g1_tiles[sy]

    g2_sy_ring.wait_recv()
    g2_sx[sx] = jnp.sum(g2_sy[...], axis=0)
    g2_sx_ring = Ring("sx", sx, N_SX, lambda peer: g2_sx.at[sx], g2_sx, g2_sx_sems)

    g1_sy_ring.wait_recv()
    g1_af[af] = jnp.sum(g1_sy[...], axis=0)
    g1_af_ring = Ring("af", af, N_AF, lambda peer: g1_af.at[af], g1_af, g1_af_sems)

    g2_sx_ring.wait_recv()
    g2_done[sy] = jnp.sum(g2_sx[...], axis=0) * (1.0 / 256.0)
    g2_done_ring = Ring("sy", sy, N_SY, lambda peer: g2_done.at[sy], g2_done, g2_done_sems)

    g1_af_ring.wait_recv()
    g1_part[sy] = jnp.sum(g1_af[...], axis=0) * (524288.0**-0.5)
    g1_part_ring = Ring("sy", sy, N_SY, lambda peer: g1_part.at[sy], g1_part, g1_part_sems)

    g2_done_ring.wait_recv()
    for k in range(27):
        half, place = k // 14, k % 14
        tile = g2_done[place // 2, 8 * half : 8 * half + 8]
        grad_two_ref[k] = tile[:, 64 * (place % 2) : 64 * (place % 2) + 64]

    g1_part_ring.wait_recv()
    g1_done_ring = Ring("sx", sx, N_SX, lambda peer: g1_part, g1_done, g1_done_sems)
    g1_done[sx] = g1_part[...]
    g1_done_ring.wait_recv()
    for k in range(27):
        for q in range(4):
            tile = g1_done[q, k // 4]
            grad_one_ref[k, 16 * q : 16 * q + 16] = tile[:, 32 * (k % 4) : 32 * (k % 4) + 32]

    for wait in pending:
        wait()


def per_device(inputs, weight_one, weight_two, cotangent):
    x = inputs.reshape(32, 2, 512).transpose(1, 0, 2)
    cot = cotangent.reshape(128, 128)
    w2 = jnp.pad(weight_two, ((0, 1), (0, 0), (0, 0)))
    w2 = w2.reshape(2, 14, 8, 64).transpose(0, 2, 1, 3).reshape(16, 896)
    vmem = pl.BlockSpec(memory_space=pltpu.VMEM)
    ring_sems = [pltpu.SemaphoreType.DMA((2, n)) for n in (16, 16, 8, 4, 8, 4, 8, 16, 8, 4)]
    output, grad_one, grad_two = pl.pallas_call(
        kernel,
        out_shape=(
            jax.ShapeDtypeStruct((128, 128), BF16),
            jax.ShapeDtypeStruct((27, 64, 32), F32),
            jax.ShapeDtypeStruct((27, 8, 64), F32),
        ),
        in_specs=[vmem] * 4,
        out_specs=(vmem, vmem, vmem),
        scratch_shapes=[
            pltpu.VMEM((4, 32, 512), BF16),
            pltpu.VMEM((64, 864), BF16),
            pltpu.VMEM((16, 16, 896), BF16),
            pltpu.VMEM((128, 128), BF16),
            pltpu.VMEM((8, 128, 128), BF16),
            pltpu.VMEM((1152, 512), BF16),
            pltpu.VMEM((2, 64, 512), F32),
            pltpu.VMEM((3, 64, 128), BF16),
            pltpu.VMEM((2, 64, 128), BF16),
            pltpu.VMEM((8, 64, 128), BF16),
            pltpu.VMEM((896, 256), BF16),
            pltpu.VMEM((3, 128, 128), BF16),
            pltpu.VMEM((2, 128, 128), BF16),
            pltpu.VMEM((8, 128, 128), BF16),
            pltpu.VMEM((64, 3584), BF16),
            pltpu.VMEM((3584, 128), BF16),
            pltpu.VMEM((16, 16, 896), BF16),
            pltpu.VMEM((16, 16, 896), BF16),
            pltpu.VMEM((8, 16, 128), F32),
            pltpu.VMEM((8, 16, 128), F32),
            pltpu.VMEM((4, 16, 128), F32),
            pltpu.VMEM((8, 16, 128), F32),
            pltpu.VMEM((64, 896), F32),
            pltpu.VMEM((4, 16, 896), BF16),
            pltpu.VMEM((4, 16, 896), BF16),
            pltpu.VMEM((8, 16, 128), F32),
            pltpu.VMEM((8, 16, 128), F32),
            pltpu.VMEM((16, 16, 128), F32),
            pltpu.VMEM((8, 16, 128), F32),
            pltpu.VMEM((4, 8, 16, 128), F32),
            pltpu.SemaphoreType.DMA((2, 3, 2)),
            pltpu.SemaphoreType.DMA((2, 3, 8)),
            *ring_sems,
        ],
        compiler_params=pltpu.CompilerParams(
            collective_id=0, has_side_effects=True, vmem_limit_bytes=48 * 2**20
        ),
    )(x, weight_one, w2, cot)
    return output.reshape(128, 1, 1, 1, 128), grad_one, grad_two


def solution(mesh):
    placed = (
        P(None, "af", "sy", "sx", None),
        P(),
        P(None, "af", None),
        P(None, "af", "sy", "sx", None),
    )
    return jax.shard_map(
        per_device,
        mesh=mesh,
        in_specs=placed,
        out_specs=(P(None, "af", "sy", "sx", None), P(), P(None, "af", None)),
        check_vma=False,
    )
```

```python
import functools

import jax
import jax.numpy as jnp
from jax import lax
from jax.experimental import pallas as pl
from jax.experimental.pallas import tpu as pltpu
from jax.sharding import PartitionSpec as P

MESH = pl.DeviceIdType.MESH
BF16 = jnp.bfloat16
F32 = jnp.float32
N_SX, N_SY, N_AF = 4, 8, 16
SLOTS = [(dx, dy) for dy in (-1, 0, 1) for dx in (-1, 0, 1) if (dx, dy) != (0, 0)]


def iota(shape, axis):
    return lax.broadcasted_iota(jnp.int32, shape, axis)


def leaky(values):
    return jnp.where(values > 0, values, 0.3 * values)


def slope(values):
    return jnp.where(values > 0, 1.0, 0.3)


def one_hot(rows, source):
    return (iota((rows, source.shape[1]), 0) == source).astype(F32).astype(BF16)


def dot(a, b):
    return jnp.dot(a, b, preferred_element_type=F32)


def dot_nt(a, b):
    return lax.dot_general(a, b, (((1,), (1,)), ((), ())), preferred_element_type=F32)


def rolled(values, shift):
    shift = shift % values.shape[1]
    return values if shift == 0 else pltpu.roll(values, shift, 1)


def border_selection_one():
    lane = iota((1, 128), 1)
    source = jnp.full((1, 128), -1, jnp.int32)
    source = jnp.where(lane == 0, 511, source)
    source = jnp.where((lane >= 1) & (lane <= 16), 32 * (lane - 1) + 31, source)
    source = jnp.where(lane == 17, 31, source)
    source = jnp.where((lane >= 32) & (lane < 64), 480 + lane - 32, source)
    source = jnp.where(lane == 64, 480, source)
    source = jnp.where((lane >= 65) & (lane <= 80), 32 * (lane - 65), source)
    source = jnp.where(lane == 81, 0, source)
    source = jnp.where(lane >= 96, lane - 96, source)
    return one_hot(512, source)


def column_placement_one():
    lane = iota((1, 1536), 1)
    offset = lane // 512
    y = lane % 512 // 32
    x = lane % 32
    source = jnp.where(x == 0, y + offset, jnp.where(x == 31, 64 + y + offset, -1))
    return one_hot(128, source)


def extension():
    lane = iota((1, 256), 1)
    y, x = lane // 20 - 2, lane % 20 - 2
    dy = jnp.where(y < 0, -1, jnp.where(y >= 8, 1, 0))
    dx = jnp.where(x < 0, -1, jnp.where(x >= 16, 1, 0))
    slot = 3 * (dy + 1) + dx + 1
    slot = jnp.where(slot == 4, 8, jnp.where(slot > 4, slot - 1, slot))
    source = 128 * slot + 16 * (y - 8 * dy) + x - 16 * dx
    return one_hot(1152, jnp.where(lane < 240, source, -1))


def interior_selection():
    lane = iota((1, 128), 1)
    return one_hot(256, 20 * (lane // 16 + 2) + lane % 16 + 2)


def pool_selection():
    lane = iota((1, 128), 1)
    return one_hot(512, 64 * (lane // 16) + 2 * (lane % 16))


def spread_selection():
    lane = iota((1, 512), 1)
    return one_hot(256, 20 * (lane // 64 + 2) + lane % 32 // 2 + 2)


def kernel(
    x_ref, w1_ref, w2_ref, cot_ref,
    out_ref, grad_one_ref, grad_two_ref,
    select_one, place_one, extend, pool_select, spread_select, interior_select,
    x_all, w1_cat, w2_own, w2_all, w2_cat, w2_turned,
    pack_one, recv_one, patches_one, hidden_one,
    p_own, p_recv, p_all, patches_two, c_recv, c_all, patches_d,
    g2_send, g2_sx, g2_part, g2_af, g2_sy, g2_done,
    g1_full, g1_send, g1_sx, g1_tiles, g1_sy, g1_af, g1_part, g1_done,
    z_sems, plane_sems, w2_sems, g2_sems, g1_sems,
):
    sx, sy, af = lax.axis_index("sx"), lax.axis_index("sy"), lax.axis_index("af")
    af_x, af_y = af % 4, af // 4

    barrier = pltpu.get_barrier_semaphore()
    for axis, me, count in (("sx", sx, N_SX), ("sy", sy, N_SY), ("af", af, N_AF)):

        def greet(j, carry, axis=axis, me=me, count=count):
            pl.semaphore_signal(
                barrier, inc=1, device_id={axis: lax.rem(me + j, count)}, device_id_type=MESH
            )
            return carry

        lax.fori_loop(1, count, greet, 0)
    for dx in (1, N_SX - 1):
        for dy in (1, N_SY - 1):
            pl.semaphore_signal(
                barrier,
                inc=1,
                device_id={"sx": lax.rem(sx + dx, N_SX), "sy": lax.rem(sy + dy, N_SY)},
                device_id_type=MESH,
            )

    x_all[1] = x_ref[0]
    x_all[2] = x_ref[1]
    for t in range(7):
        rows = []
        for half in range(2):
            pair = []
            for k in (14 * half + 2 * t, 14 * half + 2 * t + 1):
                pair.append(w2_ref[k].astype(F32) if k < 27 else jnp.zeros((8, 64), F32))
            rows.append(jnp.concatenate(pair, axis=1))
        w2_own[:, 128 * t : 128 * t + 128] = jnp.concatenate(rows, axis=0).astype(BF16)
    w2_all[af_x, af_y] = w2_own[...]
    w1_cat[...] = w1_ref[...].astype(F32).reshape(864, 64).T.astype(BF16)
    select_one[...] = border_selection_one()
    place_one[...] = column_placement_one()
    extend[...] = extension()
    pool_select[...] = pool_selection()
    spread_select[...] = spread_selection()
    interior_select[...] = interior_selection()
    patches_two[2880:2944] = jnp.zeros((64, 256), BF16)

    pl.semaphore_wait(barrier, N_SX + N_SY + N_AF + 1)

    pending = []

    class Group:
        def __init__(self, count, source, target, device, sems):
            self.count = count

            def copy(j):
                return pltpu.make_async_remote_copy(
                    src_ref=source(j),
                    dst_ref=target,
                    send_sem=sems.at[0, j],
                    recv_sem=sems.at[1, j],
                    device_id=device(j),
                    device_id_type=MESH,
                )

            self.copy = copy
            self.each(lambda copy: copy.start())
            pending.append(self.wait_send)

        def each(self, act):
            def body(j, carry):
                act(self.copy(j))
                return carry

            lax.fori_loop(1, self.count, body, 0)

        def wait_recv(self):
            self.each(lambda copy: copy.wait_recv())

        def wait_send(self):
            self.each(lambda copy: copy.wait_send())

    def ring(axis, me, count, source, target, sems):
        return Group(
            count,
            lambda j: source(lax.rem(me + j, count)),
            target.at[me],
            lambda j: {axis: lax.rem(me + j, count)},
            sems,
        )

    def exchange_planes(steps, target, sems):
        copies = []
        for way, (step, source, slot) in enumerate(steps):
            copy = pltpu.make_async_remote_copy(
                src_ref=source,
                dst_ref=target.at[slot],
                send_sem=sems.at[0, way],
                recv_sem=sems.at[1, way],
                device_id={"af": lax.rem(af + N_AF + step, N_AF)},
                device_id_type=MESH,
            )
            copy.start()
            pending.append(copy.wait_send)
            copies.append(copy)
        return copies

    def exchange_borders(source, target, sems):
        copies = []
        for slot, (dx, dy) in enumerate(SLOTS):
            copy = pltpu.make_async_remote_copy(
                src_ref=source,
                dst_ref=target.at[slot],
                send_sem=sems.at[0, slot],
                recv_sem=sems.at[1, slot],
                device_id={
                    "sx": lax.rem(sx + N_SX - dx, N_SX),
                    "sy": lax.rem(sy + N_SY - dy, N_SY),
                },
                device_id_type=MESH,
            )
            copy.start()
            pending.append(copy.wait_send)
            copies.append(copy)
        return copies

    def inside(dx, dy):
        good = True
        if dx:
            good = (sx > 0) if dx < 0 else (sx < N_SX - 1)
        if dy:
            row = (sy > 0) if dy < 0 else (sy < N_SY - 1)
            good = row if good is True else good & row
        return good

    def gather_columns(received, height, right):
        first = received[0].astype(F32)
        lane = iota(first.shape, 1)
        columns = jnp.zeros(first.shape, F32)
        for dx, start in ((-1, 0), (1, right)):
            for dy, cells in (
                (0, (lane >= start + 1) & (lane <= start + height)),
                (-1, lane == start),
                (1, lane == start + height + 1),
            ):
                values = received[SLOTS.index((dx, dy))].astype(F32)
                columns = jnp.where(cells & inside(dx, dy), values, columns)
        return columns.astype(BF16)

    def masked_rows(received, dy):
        values = received[SLOTS.index((0, dy))].astype(F32)
        return jnp.where(inside(0, dy), values, 0.0)

    def extended(received, own):
        planes = []
        for slot, (dx, dy) in enumerate(SLOTS):
            planes.append(jnp.where(inside(dx, dy), received[slot].astype(F32), 0.0).astype(BF16))
        joined = jnp.concatenate(planes + [own], axis=1)
        return dot(joined, extend[...]).astype(BF16)

    x_copies = exchange_planes(
        [(-1, x_ref.at[0], 3), (1, x_ref.at[1], 0)], x_all, z_sems.at[0]
    )
    w2_far = Group(
        4,
        lambda j: w2_own,
        w2_all.at[af_x, af_y],
        lambda j: {"af": lax.rem(af_y + j, 4) * 4 + af_x},
        w2_sems.at[0],
    )
    c_copies = exchange_borders(cot_ref, c_recv, plane_sems.at[2])
    for copy in x_copies:
        copy.wait_recv()

    field = x_all[...].reshape(128, 512).astype(F32)
    row = iota((128, 512), 0)
    outer = ((row < 32) & (af == 0)) | ((row >= 96) & (af == N_AF - 1))
    field = jnp.where(outer, 0.0, field)
    pack_one[...] = dot(field.astype(BF16), select_one[...]).astype(BF16)
    copies = exchange_borders(pack_one, recv_one, plane_sems.at[0])
    w2_far.wait_recv()
    w2_near = Group(
        4,
        lambda j: w2_all.at[af_x],
        w2_all.at[af_x],
        lambda j: {"af": af_y * 4 + lax.rem(af_x + j, 4)},
        w2_sems.at[1],
    )
    for copy in c_copies:
        copy.wait_recv()
    c_all[1] = extended(c_recv, cot_ref[...])
    for copy in copies:
        copy.wait_recv()
    columns = dot(gather_columns(recv_one, 16, 64), place_one[...])
    above, below = masked_rows(recv_one, -1), masked_rows(recv_one, 1)
    lane = iota((128, 128), 1)
    x = iota((128, 512), 1) % 32
    for b in range(3):
        for c in range(3):
            dy, dx = b - 1, c - 1
            moved = rolled(field, -(32 * dy + dx))
            if dy == -1:
                first = jnp.where(lane < 32, rolled(above, -(32 + dx)), moved[:, :128])
                moved = jnp.concatenate([first, moved[:, 128:]], axis=1)
            if dy == 1:
                final = jnp.where(lane >= 96, rolled(below, -dx), moved[:, 384:])
                moved = jnp.concatenate([moved[:, :384], final], axis=1)
            if dx:
                placed = columns[:, 512 * b : 512 * b + 512]
                moved = jnp.where(x == (0 if dx < 0 else 31), placed, moved)
            moved = moved.astype(BF16)
            start = 32 * (3 * b + c)
            for z in range(4):
                patches_one[288 * z + start : 288 * z + start + 32] = moved[32 * z : 32 * z + 32]
    total = None
    for z in range(2):
        hidden = dot(w1_cat[...], patches_one[288 * z : 288 * z + 864])
        hidden_one[z] = hidden
        total = leaky(hidden) if total is None else total + leaky(hidden)
    total = total + rolled(total, -1)
    total = total + rolled(total, -32)
    p_own[...] = dot((total * 0.125).astype(BF16), pool_select[...]).astype(BF16)

    copies = exchange_borders(p_own, p_recv, plane_sems.at[1])
    c_steps = exchange_planes(
        [(-1, c_all.at[1], 2), (1, c_all.at[1], 0)], c_all, z_sems.at[2]
    )
    w2_near.wait_recv()
    pieces = [w2_all[p % 4, p // 4].astype(F32) for p in range(16)]
    for half in range(2):
        filters = jnp.concatenate([piece[8 * half : 8 * half + 8] for piece in pieces], axis=0)
        w2_cat[half] = filters.astype(BF16)
        turned = filters.T.astype(BF16)
        for place in range(14):
            k = 14 * half + place
            if k < 27:
                start = 128 * (26 - k)
                w2_turned[:, start : start + 128] = turned[64 * place : 64 * place + 64]
    for copy in copies:
        copy.wait_recv()
    p_all[2] = extended(p_recv, p_own[...])
    copies = exchange_planes(
        [(step, p_all.at[2], 2 - step) for step in (-2, -1, 1, 2)], p_all, z_sems.at[1]
    )

    def shift_plane(values, target, start, channels):
        for b in range(3):
            for c in range(3):
                moved = rolled(values, -(20 * (b - 1) + c - 1)).astype(BF16)
                place = start + channels * (3 * b + c)
                target[place : place + channels] = moved

    shift_plane(p_all[2].astype(F32), patches_two, 576 * 2, 64)
    for z, copy in ((4, copies[0]), (3, copies[1]), (1, copies[2]), (0, copies[3])):
        copy.wait_recv()
        values = p_all[z].astype(F32)
        exists = (af + z >= 2) & (af + z < N_AF + 2)
        shift_plane(jnp.where(exists, values, 0.0), patches_two, 576 * z, 64)
    for copy in c_steps:
        copy.wait_recv()

    lane = iota((128, 256), 1)
    y, x = lane // 20 - 2, lane % 20 - 2
    own = (y >= 0) & (y < 8) & (x >= 0) & (x < 16)
    grid_y, grid_x = 8 * sy + y, 16 * sx + x
    on_grid = (grid_y >= 0) & (grid_y < 8 * N_SY) & (grid_x >= 0) & (grid_x < 16 * N_SX)
    for z in range(3):
        start = 576 * z
        hidden = dot(w2_cat[0], patches_two[start : start + 896])
        hidden = hidden + dot(w2_cat[1], patches_two[start + 896 : start + 1792])
        if z == 1:
            out_ref[...] = dot(leaky(hidden).astype(BF16), interior_select[...]).astype(BF16)
        delta = (c_all[z].astype(F32) * slope(hidden)).astype(BF16).astype(F32)
        exists = (af + z >= 1) & (af + z < N_AF + 1)
        delta = jnp.where(on_grid & exists, delta, 0.0)
        if z == 1:
            delta_two = jnp.where(own, delta, 0.0).astype(BF16)
        shift_plane(delta, patches_d, 1152 * z, 128)

    halves = []
    for half in range(2):
        start = 576 + 896 * half
        part = dot_nt(delta_two, patches_two[start : start + 896]).reshape(16, 1, 8, 896)
        halves.append(part)
    parts = jnp.concatenate(halves, axis=1).reshape(16, 16, 896).astype(BF16)
    for q in range(3):
        g2_send[q] = parts[:, :, 256 * q : 256 * q + 256]
    g2_send[3] = jnp.concatenate([parts[:, :, 768:], jnp.zeros((16, 16, 128), BF16)], axis=2)
    g2_sx_ring = ring("sx", sx, N_SX, lambda peer: g2_send.at[peer], g2_sx, g2_sems.at[0])
    g2_sx[sx] = g2_send[sx]

    pooled_grad = dot(w2_turned[...], patches_d[...]).astype(BF16)

    spread = dot(pooled_grad, spread_select[...]) * 0.125
    total = None
    for z in range(2):
        delta_one = (spread * slope(hidden_one[z])).astype(BF16)
        part = dot_nt(delta_one, patches_one[288 * z : 288 * z + 864])
        total = part if total is None else total + part
    g1_full[:, 768:] = jnp.zeros((64, 128), F32)
    g1_full[:, :864] = total
    g1_send[...] = g1_full[...].astype(BF16).reshape(4, 16, 896)
    g1_sx_ring = ring("sx", sx, N_SX, lambda peer: g1_send.at[peer], g1_sx, g1_sems.at[0])
    g1_sx[sx] = g1_send[sx]

    g2_sx_ring.wait_recv()
    g2_part[...] = jnp.sum(g2_sx[...].astype(F32), axis=0).astype(BF16)
    g2_af_ring = ring("af", af, N_AF, lambda peer: g2_part.at[peer], g2_af, g2_sems.at[1])
    g2_af[af] = g2_part[af]

    g1_sx_ring.wait_recv()
    sums = jnp.sum(g1_sx[...].astype(F32), axis=0).astype(BF16)
    for t in range(7):
        g1_tiles[t] = sums[:, 128 * t : 128 * t + 128]
    g1_tiles[7] = jnp.zeros((16, 128), BF16)
    g1_sy_ring = ring("sy", sy, N_SY, lambda peer: g1_tiles.at[peer], g1_sy, g1_sems.at[1])
    g1_sy[sy] = g1_tiles[sy]

    g1_sy_ring.wait_recv()
    g1_af[af] = jnp.sum(g1_sy[...].astype(F32), axis=0).astype(BF16)
    g1_af_ring = ring("af", af, N_AF, lambda peer: g1_af.at[af], g1_af, g1_sems.at[2])

    g2_af_ring.wait_recv()
    g2_sy[sy] = jnp.sum(g2_af[...].astype(F32), axis=0).astype(BF16)
    g2_sy_ring = ring("sy", sy, N_SY, lambda peer: g2_sy.at[sy], g2_sy, g2_sems.at[2])

    g1_af_ring.wait_recv()
    sums = jnp.sum(g1_af[...].astype(F32), axis=0) * (524288.0**-0.5)
    g1_part[sy] = sums.astype(BF16)
    g1_part_ring = ring("sy", sy, N_SY, lambda peer: g1_part.at[sy], g1_part, g1_sems.at[3])

    g2_sy_ring.wait_recv()
    sums = jnp.sum(g2_sy[...].astype(F32), axis=0) * (1.0 / 256.0)
    g2_done[sx] = sums.astype(BF16)
    g2_done_ring = ring("sx", sx, N_SX, lambda peer: g2_done.at[sx], g2_done, g2_sems.at[3])

    g1_part_ring.wait_recv()
    g1_done_ring = ring("sx", sx, N_SX, lambda peer: g1_part, g1_done, g1_sems.at[4])
    g1_done[sx] = g1_part[...]

    g2_done_ring.wait_recv()
    for k in range(27):
        half, place = k // 14, k % 14
        tile = g2_done[place // 4].astype(F32)[8 * half : 8 * half + 8]
        grad_two_ref[k] = tile[:, 64 * (place % 4) : 64 * (place % 4) + 64]

    g1_done_ring.wait_recv()
    for t in range(7):
        tile = jnp.concatenate([g1_done[q, t].astype(F32) for q in range(4)], axis=0).T
        for k in range(4 * t, min(4 * t + 4, 27)):
            grad_one_ref[k] = tile[32 * (k - 4 * t) : 32 * (k - 4 * t) + 32]

    for wait in pending:
        wait()


def per_device(inputs, weight_one, weight_two, cotangent):
    x = inputs.reshape(32, 2, 512).transpose(1, 0, 2)
    cot = cotangent.reshape(128, 128)
    vmem = pl.BlockSpec(memory_space=pltpu.VMEM)
    output, grad_one, grad_two = pl.pallas_call(
        kernel,
        out_shape=(
            jax.ShapeDtypeStruct((128, 128), BF16),
            jax.ShapeDtypeStruct((27, 32, 64), F32),
            jax.ShapeDtypeStruct((27, 8, 64), F32),
        ),
        in_specs=[vmem] * 4,
        out_specs=(vmem, vmem, vmem),
        scratch_shapes=[
            pltpu.VMEM((512, 128), BF16),
            pltpu.VMEM((128, 1536), BF16),
            pltpu.VMEM((1152, 256), BF16),
            pltpu.VMEM((512, 128), BF16),
            pltpu.VMEM((256, 512), BF16),
            pltpu.VMEM((256, 128), BF16),
            pltpu.VMEM((4, 32, 512), BF16),
            pltpu.VMEM((64, 864), BF16),
            pltpu.VMEM((16, 896), BF16),
            pltpu.VMEM((4, 4, 16, 896), BF16),
            pltpu.VMEM((2, 128, 896), BF16),
            pltpu.VMEM((64, 3456), BF16),
            pltpu.VMEM((128, 128), BF16),
            pltpu.VMEM((8, 128, 128), BF16),
            pltpu.VMEM((1152, 512), BF16),
            pltpu.VMEM((2, 64, 512), F32),
            pltpu.VMEM((64, 128), BF16),
            pltpu.VMEM((8, 64, 128), BF16),
            pltpu.VMEM((5, 64, 256), BF16),
            pltpu.VMEM((2944, 256), BF16),
            pltpu.VMEM((8, 128, 128), BF16),
            pltpu.VMEM((3, 128, 256), BF16),
            pltpu.VMEM((3456, 256), BF16),
            pltpu.VMEM((4, 16, 16, 256), BF16),
            pltpu.VMEM((4, 16, 16, 256), BF16),
            pltpu.VMEM((16, 16, 256), BF16),
            pltpu.VMEM((16, 16, 256), BF16),
            pltpu.VMEM((8, 16, 256), BF16),
            pltpu.VMEM((4, 16, 256), BF16),
            pltpu.VMEM((64, 896), F32),
            pltpu.VMEM((4, 16, 896), BF16),
            pltpu.VMEM((4, 16, 896), BF16),
            pltpu.VMEM((8, 16, 128), BF16),
            pltpu.VMEM((8, 16, 128), BF16),
            pltpu.VMEM((16, 16, 128), BF16),
            pltpu.VMEM((8, 16, 128), BF16),
            pltpu.VMEM((4, 8, 16, 128), BF16),
            pltpu.SemaphoreType.DMA((3, 2, 4)),
            pltpu.SemaphoreType.DMA((3, 2, 8)),
            pltpu.SemaphoreType.DMA((2, 2, 4)),
            pltpu.SemaphoreType.DMA((4, 2, 16)),
            pltpu.SemaphoreType.DMA((5, 2, 16)),
        ],
        compiler_params=pltpu.CompilerParams(
            collective_id=0, has_side_effects=True, vmem_limit_bytes=48 * 2**20
        ),
    )(x, weight_one.transpose(0, 2, 1), weight_two, cot)
    return output.reshape(128, 1, 1, 1, 128), grad_one.transpose(0, 2, 1), grad_two


def solution(mesh):
    placed = (
        P(None, "af", "sy", "sx", None),
        P(),
        P(None, "af", None),
        P(None, "af", "sy", "sx", None),
    )
    return jax.shard_map(
        per_device,
        mesh=mesh,
        in_specs=placed,
        out_specs=(P(None, "af", "sy", "sx", None), P(), P(None, "af", None)),
        check_vma=False,
    )
```

```python
import functools

import jax
import jax.numpy as jnp
from jax import lax
from jax.experimental import pallas as pl
from jax.experimental.pallas import tpu as pltpu
from jax.sharding import PartitionSpec as P

MESH = pl.DeviceIdType.MESH
BF16 = jnp.bfloat16
F32 = jnp.float32
N_SX, N_SY, N_AF = 4, 8, 16
SLOTS = [(dx, dy) for dy in (-1, 0, 1) for dx in (-1, 0, 1) if (dx, dy) != (0, 0)]


def iota(shape, axis):
    return lax.broadcasted_iota(jnp.int32, shape, axis)


def leaky(values):
    return jnp.where(values > 0, values, 0.3 * values)


def slope(values):
    return jnp.where(values > 0, 1.0, 0.3)


def one_hot(rows, source):
    return (iota((rows, source.shape[1]), 0) == source).astype(F32).astype(BF16)


def dot(a, b):
    return jnp.dot(a, b, preferred_element_type=F32)


def dot_nt(a, b):
    return lax.dot_general(a, b, (((1,), (1,)), ((), ())), preferred_element_type=F32)


def rolled(values, shift):
    shift = shift % values.shape[1]
    return values if shift == 0 else pltpu.roll(values, shift, 1)


def border_selection_one():
    lane = iota((1, 128), 1)
    source = jnp.full((1, 128), -1, jnp.int32)
    source = jnp.where(lane == 0, 511, source)
    source = jnp.where((lane >= 1) & (lane <= 16), 32 * (lane - 1) + 31, source)
    source = jnp.where(lane == 17, 31, source)
    source = jnp.where((lane >= 32) & (lane < 64), 480 + lane - 32, source)
    source = jnp.where(lane == 64, 480, source)
    source = jnp.where((lane >= 65) & (lane <= 80), 32 * (lane - 65), source)
    source = jnp.where(lane == 81, 0, source)
    source = jnp.where(lane >= 96, lane - 96, source)
    return one_hot(512, source)


def column_placement_one():
    lane = iota((1, 1536), 1)
    offset = lane // 512
    y = lane % 512 // 32
    x = lane % 32
    source = jnp.where(x == 0, y + offset, jnp.where(x == 31, 64 + y + offset, -1))
    return one_hot(128, source)


def extension():
    lane = iota((1, 256), 1)
    y, x = lane // 20 - 2, lane % 20 - 2
    dy = jnp.where(y < 0, -1, jnp.where(y >= 8, 1, 0))
    dx = jnp.where(x < 0, -1, jnp.where(x >= 16, 1, 0))
    slot = 3 * (dy + 1) + dx + 1
    slot = jnp.where(slot == 4, 8, jnp.where(slot > 4, slot - 1, slot))
    source = 128 * slot + 16 * (y - 8 * dy) + x - 16 * dx
    return one_hot(1152, jnp.where(lane < 240, source, -1))


def interior_selection():
    lane = iota((1, 128), 1)
    return one_hot(256, 20 * (lane // 16 + 2) + lane % 16 + 2)


def pool_selection():
    lane = iota((1, 128), 1)
    return one_hot(512, 64 * (lane // 16) + 2 * (lane % 16))


def spread_selection():
    lane = iota((1, 512), 1)
    return one_hot(256, 20 * (lane // 64 + 2) + lane % 32 // 2 + 2)


def kernel(
    x_ref, w1_ref, w2_ref, cot_ref,
    out_ref, grad_one_ref, grad_two_ref,
    select_one, place_one, extend, pool_select, spread_select, interior_select,
    x_all, w1_cat, w2_own, w2_all, w2_cat, w2_turned,
    pack_one, recv_one, patches_one, hidden_one,
    p_own, p_recv, p_all, patches_two, c_recv, c_all, patches_d,
    g2_send, g2_pair, g2_part, g2_recv, g2_tiles, g2_far, g2_sy, g2_done,
    g1_full, g1_send, g1_recv, g1_far, g1_sy, g1_done,
    z_sems, plane_sems, w2_sems, g2_sems, g1_sems,
):
    sx, sy, af = lax.axis_index("sx"), lax.axis_index("sy"), lax.axis_index("af")
    af_x, af_y = af % 4, af // 4
    core, half_y = sx % 2, sx // 2

    barrier = pltpu.get_barrier_semaphore()
    greeted = [
        {"sx": lax.rem(sx + dx, N_SX), "sy": lax.rem(sy + dy, N_SY)}
        for dx in (0, 1, N_SX - 1)
        for dy in (0, 1, N_SY - 1)
        if dx or dy
    ]
    greeted += [{"af": lax.rem(af + step, N_AF)} for step in (1, N_AF - 1)]
    greeted += [{"af": af_y * 4 + lax.rem(af_x + j, 4)} for j in (1, 2, 3)]
    greeted += [{"af": lax.rem(af_y + j, 4) * 4 + af_x} for j in (1, 2, 3)]
    greeted += [{"sy": lax.rem(sy + N_SY // 2, N_SY)}]
    for device in greeted:
        pl.semaphore_signal(barrier, inc=1, device_id=device, device_id_type=MESH)

    for t in range(7):
        rows = []
        for half in range(2):
            pair = []
            for k in (14 * half + 2 * t, 14 * half + 2 * t + 1):
                pair.append(w2_ref[k].astype(F32) if k < 27 else jnp.zeros((8, 64), F32))
            rows.append(jnp.concatenate(pair, axis=1))
        w2_own[:, 128 * t : 128 * t + 128] = jnp.concatenate(rows, axis=0).astype(BF16)
    pl.semaphore_wait(barrier, len(greeted))

    pending = []

    class Group:
        def __init__(self, count, source, target, device, sems):
            self.count = count

            def copy(j):
                return pltpu.make_async_remote_copy(
                    src_ref=source(j),
                    dst_ref=target,
                    send_sem=sems.at[0, j],
                    recv_sem=sems.at[1, j],
                    device_id=device(j),
                    device_id_type=MESH,
                )

            self.copy = copy
            self.each(lambda copy: copy.start())
            pending.append(self.wait_send)

        def each(self, act):
            def body(j, carry):
                act(self.copy(j))
                return carry

            lax.fori_loop(1, self.count, body, 0)

        def wait_recv(self):
            self.each(lambda copy: copy.wait_recv())

        def wait_send(self):
            self.each(lambda copy: copy.wait_send())

    def ring(axis, me, count, source, target, sems):
        return Group(
            count,
            lambda j: source(lax.rem(me + j, count)),
            target.at[me],
            lambda j: {axis: lax.rem(me + j, count)},
            sems,
        )

    def exchange_planes(steps, target, sems):
        copies = []
        for way, (step, source, slot) in enumerate(steps):
            copy = pltpu.make_async_remote_copy(
                src_ref=source,
                dst_ref=target.at[slot],
                send_sem=sems.at[0, way],
                recv_sem=sems.at[1, way],
                device_id={"af": lax.rem(af + N_AF + step, N_AF)},
                device_id_type=MESH,
            )
            copy.start()
            pending.append(copy.wait_send)
            copies.append(copy)
        return copies

    def exchange_borders(source, target, sems):
        copies = []
        for slot, (dx, dy) in enumerate(SLOTS):
            copy = pltpu.make_async_remote_copy(
                src_ref=source,
                dst_ref=target.at[slot],
                send_sem=sems.at[0, slot],
                recv_sem=sems.at[1, slot],
                device_id={
                    "sx": lax.rem(sx + N_SX - dx, N_SX),
                    "sy": lax.rem(sy + N_SY - dy, N_SY),
                },
                device_id_type=MESH,
            )
            copy.start()
            pending.append(copy.wait_send)
            copies.append(copy)
        return copies

    def inside(dx, dy):
        good = True
        if dx:
            good = (sx > 0) if dx < 0 else (sx < N_SX - 1)
        if dy:
            row = (sy > 0) if dy < 0 else (sy < N_SY - 1)
            good = row if good is True else good & row
        return good

    def gather_columns(received, height, right):
        first = received[0].astype(F32)
        lane = iota(first.shape, 1)
        columns = jnp.zeros(first.shape, F32)
        for dx, start in ((-1, 0), (1, right)):
            for dy, cells in (
                (0, (lane >= start + 1) & (lane <= start + height)),
                (-1, lane == start),
                (1, lane == start + height + 1),
            ):
                values = received[SLOTS.index((dx, dy))].astype(F32)
                columns = jnp.where(cells & inside(dx, dy), values, columns)
        return columns.astype(BF16)

    def masked_rows(received, dy):
        values = received[SLOTS.index((0, dy))].astype(F32)
        return jnp.where(inside(0, dy), values, 0.0)

    def extended(received, own):
        planes = []
        for slot, (dx, dy) in enumerate(SLOTS):
            planes.append(jnp.where(inside(dx, dy), received[slot].astype(F32), 0.0).astype(BF16))
        joined = jnp.concatenate(planes + [own], axis=1)
        return dot(joined, extend[...]).astype(BF16)

    x_copies = exchange_planes(
        [(-1, x_ref.at[0], 3), (1, x_ref.at[1], 0)], x_all, z_sems.at[0]
    )
    w2_far = Group(
        4,
        lambda j: w2_own,
        w2_all.at[af_x, af_y],
        lambda j: {"af": lax.rem(af_y + j, 4) * 4 + af_x},
        w2_sems.at[0],
    )
    c_copies = exchange_borders(cot_ref, c_recv, plane_sems.at[2])

    x_all[1] = x_ref[0]
    x_all[2] = x_ref[1]
    w2_all[af_x, af_y] = w2_own[...]
    select_one[...] = border_selection_one()
    place_one[...] = column_placement_one()
    w1_cat[...] = w1_ref[...].astype(F32).reshape(864, 64).T.astype(BF16)
    extend[...] = extension()
    pool_select[...] = pool_selection()
    spread_select[...] = spread_selection()
    interior_select[...] = interior_selection()
    patches_two[2880:2944] = jnp.zeros((64, 256), BF16)
    for copy in x_copies:
        copy.wait_recv()

    field = x_all[...].reshape(128, 512).astype(F32)
    row = iota((128, 512), 0)
    outer = ((row < 32) & (af == 0)) | ((row >= 96) & (af == N_AF - 1))
    field = jnp.where(outer, 0.0, field)
    pack_one[...] = dot(field.astype(BF16), select_one[...]).astype(BF16)
    copies = exchange_borders(pack_one, recv_one, plane_sems.at[0])
    w2_far.wait_recv()
    w2_near = Group(
        4,
        lambda j: w2_all.at[af_x],
        w2_all.at[af_x],
        lambda j: {"af": af_y * 4 + lax.rem(af_x + j, 4)},
        w2_sems.at[1],
    )
    for copy in c_copies:
        copy.wait_recv()
    c_all[1] = extended(c_recv, cot_ref[...])
    for copy in copies:
        copy.wait_recv()
    columns = dot(gather_columns(recv_one, 16, 64), place_one[...])
    above, below = masked_rows(recv_one, -1), masked_rows(recv_one, 1)
    lane = iota((128, 128), 1)
    x = iota((128, 512), 1) % 32
    for b in range(3):
        for c in range(3):
            dy, dx = b - 1, c - 1
            moved = rolled(field, -(32 * dy + dx))
            if dy == -1:
                first = jnp.where(lane < 32, rolled(above, -(32 + dx)), moved[:, :128])
                moved = jnp.concatenate([first, moved[:, 128:]], axis=1)
            if dy == 1:
                final = jnp.where(lane >= 96, rolled(below, -dx), moved[:, 384:])
                moved = jnp.concatenate([moved[:, :384], final], axis=1)
            if dx:
                placed = columns[:, 512 * b : 512 * b + 512]
                moved = jnp.where(x == (0 if dx < 0 else 31), placed, moved)
            moved = moved.astype(BF16)
            start = 32 * (3 * b + c)
            for z in range(4):
                patches_one[288 * z + start : 288 * z + start + 32] = moved[32 * z : 32 * z + 32]
    total = None
    for z in range(2):
        hidden = dot(w1_cat[...], patches_one[288 * z : 288 * z + 864])
        hidden_one[z] = hidden
        total = leaky(hidden) if total is None else total + leaky(hidden)
    total = total + rolled(total, -1)
    total = total + rolled(total, -32)
    p_own[...] = dot((total * 0.125).astype(BF16), pool_select[...]).astype(BF16)

    copies = exchange_borders(p_own, p_recv, plane_sems.at[1])
    c_steps = exchange_planes(
        [(-1, c_all.at[1], 2), (1, c_all.at[1], 0)], c_all, z_sems.at[2]
    )
    w2_near.wait_recv()
    pieces = [w2_all[p % 4, p // 4].astype(F32) for p in range(16)]
    for half in range(2):
        filters = jnp.concatenate([piece[8 * half : 8 * half + 8] for piece in pieces], axis=0)
        w2_cat[half] = filters.astype(BF16)
        turned = filters.T.astype(BF16)
        for place in range(14):
            k = 14 * half + place
            if k < 27:
                start = 128 * (26 - k)
                w2_turned[:, start : start + 128] = turned[64 * place : 64 * place + 64]
    for copy in copies:
        copy.wait_recv()
    p_all[2] = extended(p_recv, p_own[...])
    copies = exchange_planes(
        [(step, p_all.at[2], 2 - step) for step in (-2, -1, 1, 2)], p_all, z_sems.at[1]
    )

    def shift_plane(values, target, start, channels):
        for b in range(3):
            for c in range(3):
                moved = rolled(values, -(20 * (b - 1) + c - 1)).astype(BF16)
                place = start + channels * (3 * b + c)
                target[place : place + channels] = moved

    shift_plane(p_all[2].astype(F32), patches_two, 576 * 2, 64)
    for z, copy in ((4, copies[0]), (3, copies[1]), (1, copies[2]), (0, copies[3])):
        copy.wait_recv()
        values = p_all[z].astype(F32)
        exists = (af + z >= 2) & (af + z < N_AF + 2)
        shift_plane(jnp.where(exists, values, 0.0), patches_two, 576 * z, 64)
    for copy in c_steps:
        copy.wait_recv()

    lane = iota((128, 256), 1)
    y, x = lane // 20 - 2, lane % 20 - 2
    own = (y >= 0) & (y < 8) & (x >= 0) & (x < 16)
    grid_y, grid_x = 8 * sy + y, 16 * sx + x
    on_grid = (grid_y >= 0) & (grid_y < 8 * N_SY) & (grid_x >= 0) & (grid_x < 16 * N_SX)
    for z in range(3):
        start = 576 * z
        hidden = dot(w2_cat[0], patches_two[start : start + 896])
        hidden = hidden + dot(w2_cat[1], patches_two[start + 896 : start + 1792])
        if z == 1:
            out_ref[...] = dot(leaky(hidden).astype(BF16), interior_select[...]).astype(BF16)
        delta = (c_all[z].astype(F32) * slope(hidden)).astype(BF16).astype(F32)
        exists = (af + z >= 1) & (af + z < N_AF + 1)
        delta = jnp.where(on_grid & exists, delta, 0.0)
        if z == 1:
            delta_two = jnp.where(own, delta, 0.0).astype(BF16)
        shift_plane(delta, patches_d, 1152 * z, 128)

    halves = []
    for half in range(2):
        start = 576 + 896 * half
        part = dot_nt(delta_two, patches_two[start : start + 896]).reshape(16, 1, 8, 896)
        halves.append(part)
    parts = jnp.concatenate(halves, axis=1).reshape(16, 16, 896).astype(BF16)
    parts = jnp.concatenate([parts, jnp.zeros((16, 16, 128), BF16)], axis=2)
    for p in range(16):
        for q in range(4):
            g2_send[q % 2, q // 2, p % 4, p // 4] = parts[p][:, 256 * q : 256 * q + 256]
    g2_core = Group(
        2,
        lambda j: g2_send.at[1 - core],
        g2_pair,
        lambda j: {"sx": sx + 1 - 2 * core},
        g2_sems.at[0],
    )

    pooled_grad = dot(w2_turned[...], patches_d[...]).astype(BF16)

    spread = dot(pooled_grad, spread_select[...]) * 0.125
    total = None
    for z in range(2):
        delta_one = (spread * slope(hidden_one[z])).astype(BF16)
        part = dot_nt(delta_one, patches_one[288 * z : 288 * z + 864])
        total = part if total is None else total + part
    g1_full[:, 768:] = jnp.zeros((64, 256), F32)
    g1_full[:, :864] = total
    sums = g1_full[...].astype(BF16)
    for q in range(4):
        for t in range(4):
            g1_send[q, t] = sums[16 * q : 16 * q + 16, 256 * t : 256 * t + 256]

    def near(j):
        return lax.rem(sx + j // 4, N_SX), lax.rem(af_x + j % 4, 4)

    def near_device(j):
        return {"sx": near(j)[0], "af": af_y * 4 + near(j)[1]}

    def far_device(j):
        return {"af": lax.rem(af_y + j, 4) * 4 + af_x}

    g1_near = Group(16, lambda j: g1_send.at[near(j)], g1_recv.at[sx, af_x], near_device, g1_sems.at[0])
    g1_recv[sx, af_x] = g1_send[sx, af_x]

    g2_core.wait_recv()
    mine = g2_send[core].astype(F32) + g2_pair[...].astype(F32)
    g2_part[...] = mine.astype(BF16)

    def beside(j):
        return lax.rem(half_y + j // 4, 2), lax.rem(af_x + j % 4, 4)

    g2_near = Group(
        8,
        lambda j: g2_part.at[beside(j)],
        g2_recv.at[half_y, af_x],
        lambda j: {"sx": beside(j)[0] * 2 + core, "af": af_y * 4 + beside(j)[1]},
        g2_sems.at[1],
    )
    g2_recv[half_y, af_x] = g2_part[half_y, af_x]

    g1_near.wait_recv()
    g1_far[af_y] = jnp.sum(g1_recv[...].astype(F32).reshape(16, 16, 256), axis=0).astype(BF16)
    g1_far_group = Group(4, lambda j: g1_far.at[af_y], g1_far.at[af_y], far_device, g1_sems.at[1])

    g2_near.wait_recv()
    sums = jnp.sum(g2_recv[...].astype(F32).reshape(8, 4, 16, 256), axis=0)
    g2_tiles[...] = sums.astype(BF16)
    g2_far_group = Group(
        4,
        lambda j: g2_tiles.at[lax.rem(af_y + j, 4)],
        g2_far.at[af_y],
        far_device,
        g2_sems.at[2],
    )
    g2_far[af_y] = g2_tiles[af_y]

    g1_far_group.wait_recv()
    g1_sy[sy] = jnp.sum(g1_far[...].astype(F32), axis=0).astype(BF16)
    g1_sy_ring = ring("sy", sy, N_SY, lambda peer: g1_sy.at[sy], g1_sy, g1_sems.at[2])

    g2_far_group.wait_recv()
    g2_sy[sy] = jnp.sum(g2_far[...].astype(F32), axis=0).astype(BF16)
    g2_sy_ring = ring("sy", sy, N_SY, lambda peer: g2_sy.at[sy], g2_sy, g2_sems.at[3])

    g1_sy_ring.wait_recv()
    sums = jnp.sum(g1_sy[...].astype(F32), axis=0) * (524288.0**-0.5)
    g1_done[sx, af_x] = sums.astype(BF16)
    g1_done_group = Group(
        16,
        lambda j: g1_done.at[sx, af_x],
        g1_done.at[sx, af_x],
        near_device,
        g1_sems.at[3],
    )

    g2_sy_ring.wait_recv()
    sums = jnp.sum(g2_sy[...].astype(F32), axis=0) * (1.0 / 256.0)
    g2_done[sx] = sums.astype(BF16)
    g2_done_ring = ring("sx", sx, N_SX, lambda peer: g2_done.at[sx], g2_done, g2_sems.at[4])

    g2_done_ring.wait_recv()
    for k in range(27):
        half, place = k // 14, k % 14
        q = place // 4
        tile = g2_done[q].astype(F32)[8 * half : 8 * half + 8]
        grad_two_ref[k] = tile[:, 64 * (place % 4) : 64 * (place % 4) + 64]

    g1_done_group.wait_recv()
    for t in range(7):
        rows = [
            g1_done[q, t // 2].astype(F32)[:, 128 * (t % 2) : 128 * (t % 2) + 128]
            for q in range(4)
        ]
        tile = jnp.concatenate(rows, axis=0).T
        for k in range(4 * t, min(4 * t + 4, 27)):
            grad_one_ref[k] = tile[32 * (k - 4 * t) : 32 * (k - 4 * t) + 32]

    for wait in pending:
        wait()


def per_device(inputs, weight_one, weight_two, cotangent):
    x = inputs.reshape(32, 2, 512).transpose(1, 0, 2)
    cot = cotangent.reshape(128, 128)
    vmem = pl.BlockSpec(memory_space=pltpu.VMEM)
    output, grad_one, grad_two = pl.pallas_call(
        kernel,
        out_shape=(
            jax.ShapeDtypeStruct((128, 128), BF16),
            jax.ShapeDtypeStruct((27, 32, 64), F32),
            jax.ShapeDtypeStruct((27, 8, 64), F32),
        ),
        in_specs=[vmem] * 4,
        out_specs=(vmem, vmem, vmem),
        scratch_shapes=[
            pltpu.VMEM((512, 128), BF16),
            pltpu.VMEM((128, 1536), BF16),
            pltpu.VMEM((1152, 256), BF16),
            pltpu.VMEM((512, 128), BF16),
            pltpu.VMEM((256, 512), BF16),
            pltpu.VMEM((256, 128), BF16),
            pltpu.VMEM((4, 32, 512), BF16),
            pltpu.VMEM((64, 864), BF16),
            pltpu.VMEM((16, 896), BF16),
            pltpu.VMEM((4, 4, 16, 896), BF16),
            pltpu.VMEM((2, 128, 896), BF16),
            pltpu.VMEM((64, 3456), BF16),
            pltpu.VMEM((128, 128), BF16),
            pltpu.VMEM((8, 128, 128), BF16),
            pltpu.VMEM((1152, 512), BF16),
            pltpu.VMEM((2, 64, 512), F32),
            pltpu.VMEM((64, 128), BF16),
            pltpu.VMEM((8, 64, 128), BF16),
            pltpu.VMEM((5, 64, 256), BF16),
            pltpu.VMEM((2944, 256), BF16),
            pltpu.VMEM((8, 128, 128), BF16),
            pltpu.VMEM((3, 128, 256), BF16),
            pltpu.VMEM((3456, 256), BF16),
            pltpu.VMEM((2, 2, 4, 4, 16, 256), BF16),
            pltpu.VMEM((2, 4, 4, 16, 256), BF16),
            pltpu.VMEM((2, 4, 4, 16, 256), BF16),
            pltpu.VMEM((2, 4, 4, 16, 256), BF16),
            pltpu.VMEM((4, 16, 256), BF16),
            pltpu.VMEM((4, 16, 256), BF16),
            pltpu.VMEM((8, 16, 256), BF16),
            pltpu.VMEM((4, 16, 256), BF16),
            pltpu.VMEM((64, 1024), F32),
            pltpu.VMEM((4, 4, 16, 256), BF16),
            pltpu.VMEM((4, 4, 16, 256), BF16),
            pltpu.VMEM((4, 16, 256), BF16),
            pltpu.VMEM((8, 16, 256), BF16),
            pltpu.VMEM((4, 4, 16, 256), BF16),
            pltpu.SemaphoreType.DMA((3, 2, 4)),
            pltpu.SemaphoreType.DMA((3, 2, 8)),
            pltpu.SemaphoreType.DMA((2, 2, 4)),
            pltpu.SemaphoreType.DMA((5, 2, 8)),
            pltpu.SemaphoreType.DMA((4, 2, 16)),
        ],
        compiler_params=pltpu.CompilerParams(
            collective_id=0, has_side_effects=True, vmem_limit_bytes=48 * 2**20
        ),
    )(x, weight_one.transpose(0, 2, 1), weight_two, cot)
    return output.reshape(128, 1, 1, 1, 128), grad_one.transpose(0, 2, 1), grad_two


def solution(mesh):
    placed = (
        P(None, "af", "sy", "sx", None),
        P(),
        P(None, "af", None),
        P(None, "af", "sy", "sx", None),
    )
    return jax.shard_map(
        per_device,
        mesh=mesh,
        in_specs=placed,
        out_specs=(P(None, "af", "sy", "sx", None), P(), P(None, "af", None)),
        check_vma=False,
    )
```

```python
import functools

import jax
import jax.numpy as jnp
from jax import lax
from jax.experimental import pallas as pl
from jax.experimental.pallas import tpu as pltpu
from jax.sharding import PartitionSpec as P

MESH = pl.DeviceIdType.MESH
BF16 = jnp.bfloat16
F32 = jnp.float32
N_SX, N_SY, N_AF = 4, 8, 16
SLOTS = [(dx, dy) for dy in (-1, 0, 1) for dx in (-1, 0, 1) if (dx, dy) != (0, 0)]


def iota(shape, axis):
    return lax.broadcasted_iota(jnp.int32, shape, axis)


def leaky(values):
    return jnp.where(values > 0, values, 0.3 * values)


def slope(values):
    return jnp.where(values > 0, 1.0, 0.3)


def one_hot(rows, source):
    return (iota((rows, source.shape[1]), 0) == source).astype(F32).astype(BF16)


def dot(a, b):
    return jnp.dot(a, b, preferred_element_type=F32)


def dot_nt(a, b):
    return lax.dot_general(a, b, (((1,), (1,)), ((), ())), preferred_element_type=F32)


def rolled(values, shift):
    shift = shift % values.shape[1]
    return values if shift == 0 else pltpu.roll(values, shift, 1)


def border_selection_one():
    lane = iota((1, 128), 1)
    source = jnp.full((1, 128), -1, jnp.int32)
    source = jnp.where(lane == 0, 511, source)
    source = jnp.where((lane >= 1) & (lane <= 16), 32 * (lane - 1) + 31, source)
    source = jnp.where(lane == 17, 31, source)
    source = jnp.where((lane >= 32) & (lane < 64), 480 + lane - 32, source)
    source = jnp.where(lane == 64, 480, source)
    source = jnp.where((lane >= 65) & (lane <= 80), 32 * (lane - 65), source)
    source = jnp.where(lane == 81, 0, source)
    source = jnp.where(lane >= 96, lane - 96, source)
    return one_hot(512, source)


def column_placement_one():
    lane = iota((1, 1536), 1)
    offset = lane // 512
    y = lane % 512 // 32
    x = lane % 32
    source = jnp.where(x == 0, y + offset, jnp.where(x == 31, 64 + y + offset, -1))
    return one_hot(128, source)


def extension():
    lane = iota((1, 256), 1)
    y, x = lane // 20 - 2, lane % 20 - 2
    dy = jnp.where(y < 0, -1, jnp.where(y >= 8, 1, 0))
    dx = jnp.where(x < 0, -1, jnp.where(x >= 16, 1, 0))
    slot = 3 * (dy + 1) + dx + 1
    slot = jnp.where(slot == 4, 8, jnp.where(slot > 4, slot - 1, slot))
    source = 128 * slot + 16 * (y - 8 * dy) + x - 16 * dx
    return one_hot(1152, jnp.where(lane < 240, source, -1))


def interior_selection():
    lane = iota((1, 128), 1)
    return one_hot(256, 20 * (lane // 16 + 2) + lane % 16 + 2)


def pool_selection():
    lane = iota((1, 128), 1)
    return one_hot(512, 64 * (lane // 16) + 2 * (lane % 16))


def spread_selection():
    lane = iota((1, 512), 1)
    return one_hot(256, 20 * (lane // 64 + 2) + lane % 32 // 2 + 2)


def kernel(
    x_ref, w1_ref, w2_ref, cot_ref,
    out_ref, one_ref, two_ref,
    select_one, place_one, extend, pool_select, spread_select, interior_select,
    x_all, w1_cat, w2_own, w2_all, w2_cat, w2_turned,
    pack_one, recv_one, patches_one, hidden_one,
    p_own, p_recv, p_all, patches_two, c_recv, c_all, patches_d,
    g2_send, g2_pair, g2_part, g2_recv, g2_tiles, g2_far, g2_done,
    g1_send, g1_recv, g1_far, g1_done, both,
    z_sems, plane_sems, w2_sems, g2_sems, g1_sems,
):
    sx, sy, af = lax.axis_index("sx"), lax.axis_index("sy"), lax.axis_index("af")
    af_x, af_y = af % 4, af // 4
    core, half_y = sx % 2, sx // 2

    barrier = pltpu.get_barrier_semaphore()
    greeted = [
        {"sx": lax.rem(sx + dx, N_SX), "sy": lax.rem(sy + dy, N_SY)}
        for dx in (0, 1, N_SX - 1)
        for dy in (0, 1, N_SY - 1)
        if dx or dy
    ]
    greeted += [{"af": lax.rem(af + step, N_AF)} for step in (1, N_AF - 1)]
    greeted += [{"af": af_y * 4 + lax.rem(af_x + j, 4)} for j in (1, 2, 3)]
    greeted += [{"af": lax.rem(af_y + j, 4) * 4 + af_x} for j in (1, 2, 3)]
    greeted += [{"sy": lax.rem(sy + N_SY // 2, N_SY)}]
    for device in greeted:
        pl.semaphore_signal(barrier, inc=1, device_id=device, device_id_type=MESH)

    x_raw = x_ref[...].astype(F32)
    x_all[1] = x_raw[:, 0].astype(BF16)
    x_all[2] = x_raw[:, 1].astype(BF16)
    for t in range(7):
        rows = []
        for half in range(2):
            pair = []
            for k in (14 * half + 2 * t, 14 * half + 2 * t + 1):
                pair.append(w2_ref[k].astype(F32) if k < 27 else jnp.zeros((8, 64), F32))
            rows.append(jnp.concatenate(pair, axis=1))
        w2_own[:, 128 * t : 128 * t + 128] = jnp.concatenate(rows, axis=0).astype(BF16)
    pl.semaphore_wait(barrier, len(greeted))

    pending = []

    class Group:
        def __init__(self, count, source, target, device, sems):
            self.count = count

            def copy(j):
                return pltpu.make_async_remote_copy(
                    src_ref=source(j),
                    dst_ref=target,
                    send_sem=sems.at[0, j],
                    recv_sem=sems.at[1, j],
                    device_id=device(j),
                    device_id_type=MESH,
                )

            self.copy = copy
            self.each(lambda copy: copy.start())
            pending.append(self.wait_send)

        def each(self, act):
            for j in range(1, self.count):
                act(self.copy(j))

        def wait_recv(self):
            self.each(lambda copy: copy.wait_recv())

        def wait_send(self):
            self.each(lambda copy: copy.wait_send())

    def ring(axis, me, count, source, target, sems):
        return Group(
            count,
            lambda j: source(lax.rem(me + j, count)),
            target.at[me],
            lambda j: {axis: lax.rem(me + j, count)},
            sems,
        )

    def exchange_planes(steps, target, sems):
        copies = []
        for way, (step, source, slot) in enumerate(steps):
            copy = pltpu.make_async_remote_copy(
                src_ref=source,
                dst_ref=target.at[slot],
                send_sem=sems.at[0, way],
                recv_sem=sems.at[1, way],
                device_id={"af": lax.rem(af + N_AF + step, N_AF)},
                device_id_type=MESH,
            )
            copy.start()
            pending.append(copy.wait_send)
            copies.append(copy)
        return copies

    def exchange_borders(source, target, sems):
        copies = []
        for slot, (dx, dy) in enumerate(SLOTS):
            copy = pltpu.make_async_remote_copy(
                src_ref=source,
                dst_ref=target.at[slot],
                send_sem=sems.at[0, slot],
                recv_sem=sems.at[1, slot],
                device_id={
                    "sx": lax.rem(sx + N_SX - dx, N_SX),
                    "sy": lax.rem(sy + N_SY - dy, N_SY),
                },
                device_id_type=MESH,
            )
            copy.start()
            pending.append(copy.wait_send)
            copies.append(copy)
        return copies

    def inside(dx, dy):
        good = True
        if dx:
            good = (sx > 0) if dx < 0 else (sx < N_SX - 1)
        if dy:
            row = (sy > 0) if dy < 0 else (sy < N_SY - 1)
            good = row if good is True else good & row
        return good

    def gather_columns(received, height, right):
        first = received[0].astype(F32)
        lane = iota(first.shape, 1)
        columns = jnp.zeros(first.shape, F32)
        for dx, start in ((-1, 0), (1, right)):
            for dy, cells in (
                (0, (lane >= start + 1) & (lane <= start + height)),
                (-1, lane == start),
                (1, lane == start + height + 1),
            ):
                values = received[SLOTS.index((dx, dy))].astype(F32)
                columns = jnp.where(cells & inside(dx, dy), values, columns)
        return columns.astype(BF16)

    def masked_rows(received, dy):
        values = received[SLOTS.index((0, dy))].astype(F32)
        return jnp.where(inside(0, dy), values, 0.0)

    def extended(received, own):
        planes = []
        for slot, (dx, dy) in enumerate(SLOTS):
            planes.append(jnp.where(inside(dx, dy), received[slot].astype(F32), 0.0).astype(BF16))
        joined = jnp.concatenate(planes + [own], axis=1)
        return dot(joined, extend[...]).astype(BF16)

    x_copies = exchange_planes(
        [(-1, x_all.at[1], 3), (1, x_all.at[2], 0)], x_all, z_sems.at[0]
    )
    w2_far = Group(
        4,
        lambda j: w2_own,
        w2_all.at[af_x, af_y],
        lambda j: {"af": lax.rem(af_y + j, 4) * 4 + af_x},
        w2_sems.at[0],
    )
    c_copies = exchange_borders(cot_ref, c_recv, plane_sems.at[2])

    w2_all[af_x, af_y] = w2_own[...]
    select_one[...] = border_selection_one()
    place_one[...] = column_placement_one()
    w1_cat[...] = w1_ref[...].astype(F32).reshape(864, 64).T.astype(BF16)
    extend[...] = extension()
    pool_select[...] = pool_selection()
    spread_select[...] = spread_selection()
    interior_select[...] = interior_selection()
    patches_two[2880:2944] = jnp.zeros((64, 256), BF16)
    for copy in x_copies:
        copy.wait_recv()

    field = x_all[...].reshape(128, 512).astype(F32)
    row = iota((128, 512), 0)
    outer = ((row < 32) & (af == 0)) | ((row >= 96) & (af == N_AF - 1))
    field = jnp.where(outer, 0.0, field)
    pack_one[...] = dot(field.astype(BF16), select_one[...]).astype(BF16)
    copies = exchange_borders(pack_one, recv_one, plane_sems.at[0])
    w2_far.wait_recv()
    w2_near = Group(
        4,
        lambda j: w2_all.at[af_x],
        w2_all.at[af_x],
        lambda j: {"af": af_y * 4 + lax.rem(af_x + j, 4)},
        w2_sems.at[1],
    )
    for copy in c_copies:
        copy.wait_recv()
    c_all[1] = extended(c_recv, cot_ref[...])
    for copy in copies:
        copy.wait_recv()
    columns = dot(gather_columns(recv_one, 16, 64), place_one[...])
    above, below = masked_rows(recv_one, -1), masked_rows(recv_one, 1)
    lane = iota((128, 128), 1)
    x = iota((128, 512), 1) % 32
    for b in range(3):
        for c in range(3):
            dy, dx = b - 1, c - 1
            moved = rolled(field, -(32 * dy + dx))
            if dy == -1:
                first = jnp.where(lane < 32, rolled(above, -(32 + dx)), moved[:, :128])
                moved = jnp.concatenate([first, moved[:, 128:]], axis=1)
            if dy == 1:
                final = jnp.where(lane >= 96, rolled(below, -dx), moved[:, 384:])
                moved = jnp.concatenate([moved[:, :384], final], axis=1)
            if dx:
                placed = columns[:, 512 * b : 512 * b + 512]
                moved = jnp.where(x == (0 if dx < 0 else 31), placed, moved)
            moved = moved.astype(BF16)
            start = 32 * (3 * b + c)
            for z in range(4):
                patches_one[288 * z + start : 288 * z + start + 32] = moved[32 * z : 32 * z + 32]
    total = None
    for z in range(2):
        hidden = dot(w1_cat[...], patches_one[288 * z : 288 * z + 864])
        hidden_one[z] = hidden
        total = leaky(hidden) if total is None else total + leaky(hidden)
    total = total + rolled(total, -1)
    total = total + rolled(total, -32)
    p_own[...] = dot((total * 0.125).astype(BF16), pool_select[...]).astype(BF16)

    copies = exchange_borders(p_own, p_recv, plane_sems.at[1])
    c_steps = exchange_planes(
        [(-1, c_all.at[1], 2), (1, c_all.at[1], 0)], c_all, z_sems.at[2]
    )
    w2_near.wait_recv()
    pieces = [w2_all[p % 4, p // 4].astype(F32) for p in range(16)]
    for half in range(2):
        filters = jnp.concatenate([piece[8 * half : 8 * half + 8] for piece in pieces], axis=0)
        w2_cat[half] = filters.astype(BF16)
        turned = filters.T.astype(BF16)
        for place in range(14):
            k = 14 * half + place
            if k < 27:
                start = 128 * (26 - k)
                w2_turned[:, start : start + 128] = turned[64 * place : 64 * place + 64]
    for copy in copies:
        copy.wait_recv()
    p_all[2] = extended(p_recv, p_own[...])
    copies = exchange_planes(
        [(step, p_all.at[2], 2 - step) for step in (-2, -1, 1, 2)], p_all, z_sems.at[1]
    )

    def shift_plane(values, target, start, channels):
        for b in range(3):
            for c in range(3):
                moved = rolled(values, -(20 * (b - 1) + c - 1)).astype(BF16)
                place = start + channels * (3 * b + c)
                target[place : place + channels] = moved

    shift_plane(p_all[2].astype(F32), patches_two, 576 * 2, 64)
    for z, copy in ((4, copies[0]), (3, copies[1]), (1, copies[2]), (0, copies[3])):
        copy.wait_recv()
        values = p_all[z].astype(F32)
        exists = (af + z >= 2) & (af + z < N_AF + 2)
        shift_plane(jnp.where(exists, values, 0.0), patches_two, 576 * z, 64)
    for copy in c_steps:
        copy.wait_recv()

    lane = iota((128, 256), 1)
    y, x = lane // 20 - 2, lane % 20 - 2
    own = (y >= 0) & (y < 8) & (x >= 0) & (x < 16)
    grid_y, grid_x = 8 * sy + y, 16 * sx + x
    on_grid = (grid_y >= 0) & (grid_y < 8 * N_SY) & (grid_x >= 0) & (grid_x < 16 * N_SX)
    for z in range(3):
        start = 576 * z
        hidden = dot(w2_cat[0], patches_two[start : start + 896])
        hidden = hidden + dot(w2_cat[1], patches_two[start + 896 : start + 1792])
        if z == 1:
            out_ref[...] = dot(leaky(hidden).astype(BF16), interior_select[...]).astype(BF16)
        delta = (c_all[z].astype(F32) * slope(hidden)).astype(BF16).astype(F32)
        exists = (af + z >= 1) & (af + z < N_AF + 1)
        delta = jnp.where(on_grid & exists, delta, 0.0)
        if z == 1:
            delta_two = jnp.where(own, delta, 0.0).astype(BF16)
        shift_plane(delta, patches_d, 1152 * z, 128)

    halves = []
    for half in range(2):
        start = 576 + 896 * half
        part = dot_nt(delta_two, patches_two[start : start + 896]).reshape(16, 1, 8, 896)
        halves.append(part)
    parts = jnp.concatenate(halves, axis=1).reshape(16, 16, 896).astype(BF16)
    parts = jnp.concatenate([parts, jnp.zeros((16, 16, 128), BF16)], axis=2)
    for p in range(16):
        for q in range(4):
            g2_send[q % 2, q // 2, p % 4, p // 4] = parts[p][:, 256 * q : 256 * q + 256]
    g2_core = Group(
        2,
        lambda j: g2_send.at[1 - core],
        g2_pair,
        lambda j: {"sx": sx + 1 - 2 * core},
        g2_sems.at[0],
    )

    pooled_grad = dot(w2_turned[...], patches_d[...]).astype(BF16)

    spread = dot(pooled_grad, spread_select[...]) * 0.125
    total = None
    for z in range(2):
        delta_one = (spread * slope(hidden_one[z])).T.astype(BF16)
        part = dot(patches_one[288 * z : 288 * z + 864], delta_one)
        total = part if total is None else total + part
    rest = jnp.concatenate([total[512:], jnp.zeros((160, 64), F32)], axis=0)
    sums = jnp.concatenate([total[:512], rest], axis=1).astype(BF16)
    g1_send[...] = sums.reshape(4, 4, 32, 128)

    def near(j):
        return lax.rem(sx + j // 4, N_SX), lax.rem(af_x + j % 4, 4)

    def near_device(j):
        return {"sx": near(j)[0], "af": af_y * 4 + near(j)[1]}

    def far_device(j):
        return {"af": lax.rem(af_y + j, 4) * 4 + af_x}

    g1_near = Group(16, lambda j: g1_send.at[near(j)], g1_recv.at[sx, af_x], near_device, g1_sems.at[0])
    g1_recv[sx, af_x] = g1_send[sx, af_x]

    g2_core.wait_recv()
    mine = g2_send[core].astype(F32) + g2_pair[...].astype(F32)
    g2_part[...] = mine.astype(BF16)

    def beside(j):
        return lax.rem(half_y + j // 4, 2), lax.rem(af_x + j % 4, 4)

    g2_near = Group(
        8,
        lambda j: g2_part.at[beside(j)],
        g2_recv.at[half_y, af_x],
        lambda j: {"sx": beside(j)[0] * 2 + core, "af": af_y * 4 + beside(j)[1]},
        g2_sems.at[1],
    )
    g2_recv[half_y, af_x] = g2_part[half_y, af_x]

    g1_near.wait_recv()
    g1_far[af_y] = jnp.sum(g1_recv[...].astype(F32).reshape(16, 32, 128), axis=0).astype(BF16)
    g1_far_group = Group(4, lambda j: g1_far.at[af_y], g1_far.at[af_y], far_device, g1_sems.at[1])

    g2_near.wait_recv()
    sums = jnp.sum(g2_recv[...].astype(F32).reshape(8, 4, 16, 256), axis=0)
    g2_tiles[...] = sums.astype(BF16)
    g2_far_group = Group(
        4,
        lambda j: g2_tiles.at[lax.rem(af_y + j, 4)],
        g2_far.at[af_y],
        far_device,
        g2_sems.at[2],
    )
    g2_far[af_y] = g2_tiles[af_y]

    g1_far_group.wait_recv()
    both[sy, 0] = jnp.sum(g1_far[...].astype(F32), axis=0).astype(BF16)

    def along_sy(j):
        return {"sy": lax.rem(sy + j, N_SY)}

    g1_sy_group = Group(N_SY, lambda j: both.at[sy, 0], both.at[sy, 0], along_sy, g1_sems.at[3])
    g2_far_group.wait_recv()
    sums = jnp.sum(g2_far[...].astype(F32), axis=0).astype(BF16)
    both[sy, 1, :16] = sums[:, :128]
    both[sy, 1, 16:] = sums[:, 128:]
    g2_sy_group = Group(N_SY, lambda j: both.at[sy, 1], both.at[sy, 1], along_sy, g2_sems.at[4])
    g1_sy_group.wait_recv()
    sums = jnp.sum(both[:, 0].astype(F32), axis=0)
    g1_done[sx, af_x] = (sums * 524288.0**-0.5).astype(BF16)
    g1_done_group = Group(
        16,
        lambda j: g1_done.at[sx, af_x],
        g1_done.at[sx, af_x],
        near_device,
        g1_sems.at[2],
    )
    g2_sy_group.wait_recv()
    sums = jnp.sum(both[:, 1].astype(F32), axis=0)
    g2_done[sx] = (sums * (1.0 / 256.0)).astype(BF16)
    g2_done_ring = ring("sx", sx, N_SX, lambda peer: g2_done.at[sx], g2_done, g2_sems.at[3])
    g2_done_ring.wait_recv()
    two_ref[...] = g2_done[...]
    g1_done_group.wait_recv()
    one_ref[...] = g1_done[...].reshape(16, 32, 128)

    for wait in pending:
        wait()


def unpack(output, one, two, output_ref, grad_one_ref, grad_two_ref):
    output_ref[...] = output[...]
    for k in range(27):
        half = 64 * (k // 16)
        grad_one_ref[k] = one[k % 16].astype(F32)[:, half : half + 64]
        half, place = k // 14, k % 14
        tile = two[place // 4].astype(F32)
        row, column = 16 * (place % 4 // 2) + 8 * half, 64 * (place % 2)
        grad_two_ref[k] = tile[row : row + 8, column : column + 64]


def per_device(inputs, weight_one, weight_two, cotangent):
    x = inputs.reshape(32, 2, 512)
    cot = cotangent.reshape(128, 128)
    vmem = pl.BlockSpec(memory_space=pltpu.VMEM)
    output, one, two = pl.pallas_call(
        kernel,
        out_shape=(
            jax.ShapeDtypeStruct((128, 128), BF16),
            jax.ShapeDtypeStruct((16, 32, 128), BF16),
            jax.ShapeDtypeStruct((4, 32, 128), BF16),
        ),
        in_specs=[vmem] * 4,
        out_specs=(vmem, vmem, vmem),
        scratch_shapes=[
            pltpu.VMEM((512, 128), BF16),
            pltpu.VMEM((128, 1536), BF16),
            pltpu.VMEM((1152, 256), BF16),
            pltpu.VMEM((512, 128), BF16),
            pltpu.VMEM((256, 512), BF16),
            pltpu.VMEM((256, 128), BF16),
            pltpu.VMEM((4, 32, 512), BF16),
            pltpu.VMEM((64, 864), BF16),
            pltpu.VMEM((16, 896), BF16),
            pltpu.VMEM((4, 4, 16, 896), BF16),
            pltpu.VMEM((2, 128, 896), BF16),
            pltpu.VMEM((64, 3456), BF16),
            pltpu.VMEM((128, 128), BF16),
            pltpu.VMEM((8, 128, 128), BF16),
            pltpu.VMEM((1152, 512), BF16),
            pltpu.VMEM((2, 64, 512), F32),
            pltpu.VMEM((64, 128), BF16),
            pltpu.VMEM((8, 64, 128), BF16),
            pltpu.VMEM((5, 64, 256), BF16),
            pltpu.VMEM((2944, 256), BF16),
            pltpu.VMEM((8, 128, 128), BF16),
            pltpu.VMEM((3, 128, 256), BF16),
            pltpu.VMEM((3456, 256), BF16),
            pltpu.VMEM((2, 2, 4, 4, 16, 256), BF16),
            pltpu.VMEM((2, 4, 4, 16, 256), BF16),
            pltpu.VMEM((2, 4, 4, 16, 256), BF16),
            pltpu.VMEM((2, 4, 4, 16, 256), BF16),
            pltpu.VMEM((4, 16, 256), BF16),
            pltpu.VMEM((4, 16, 256), BF16),
            pltpu.VMEM((4, 32, 128), BF16),
            pltpu.VMEM((4, 4, 32, 128), BF16),
            pltpu.VMEM((4, 4, 32, 128), BF16),
            pltpu.VMEM((4, 32, 128), BF16),
            pltpu.VMEM((4, 4, 32, 128), BF16),
            pltpu.VMEM((8, 2, 32, 128), BF16),
            pltpu.SemaphoreType.DMA((3, 2, 4)),
            pltpu.SemaphoreType.DMA((3, 2, 8)),
            pltpu.SemaphoreType.DMA((2, 2, 4)),
            pltpu.SemaphoreType.DMA((5, 2, 8)),
            pltpu.SemaphoreType.DMA((4, 2, 16)),
        ],
        compiler_params=pltpu.CompilerParams(
            collective_id=0, has_side_effects=True, vmem_limit_bytes=48 * 2**20
        ),
    )(x, weight_one.transpose(0, 2, 1), weight_two, cot)
    output, grad_one, grad_two = pl.pallas_call(
        unpack,
        out_shape=(
            jax.ShapeDtypeStruct((128, 128), BF16),
            jax.ShapeDtypeStruct((27, 32, 64), F32),
            jax.ShapeDtypeStruct((27, 8, 64), F32),
        ),
        in_specs=[vmem] * 3,
        out_specs=(vmem, vmem, vmem),
        compiler_params=pltpu.CompilerParams(vmem_limit_bytes=16 * 2**20),
    )(output, one, two)
    return output.reshape(128, 1, 1, 1, 128), grad_one.transpose(0, 2, 1), grad_two


def solution(mesh):
    placed = (
        P(None, "af", "sy", "sx", None),
        P(),
        P(None, "af", None),
        P(None, "af", "sy", "sx", None),
    )
    return jax.shard_map(
        per_device,
        mesh=mesh,
        in_specs=placed,
        out_specs=(P(None, "af", "sy", "sx", None), P(), P(None, "af", None)),
        check_vma=False,
    )
```

```python
import functools

import jax
import jax.numpy as jnp
from jax import lax
from jax.experimental import pallas as pl
from jax.experimental.pallas import tpu as pltpu
from jax.sharding import PartitionSpec as P

MESH = pl.DeviceIdType.MESH
BF16 = jnp.bfloat16
F32 = jnp.float32
N_SX, N_SY, N_AF = 4, 8, 16
SLOTS = [(dx, dy) for dy in (-1, 0, 1) for dx in (-1, 0, 1) if (dx, dy) != (0, 0)]


def iota(shape, axis):
    return lax.broadcasted_iota(jnp.int32, shape, axis)


def leaky(values):
    return jnp.where(values > 0, values, 0.3 * values)


def slope(values):
    return jnp.where(values > 0, 1.0, 0.3)


def one_hot(rows, source):
    return (iota((rows, source.shape[1]), 0) == source).astype(F32).astype(BF16)


def dot(a, b):
    return jnp.dot(a, b, preferred_element_type=F32)


def dot_nt(a, b):
    return lax.dot_general(a, b, (((1,), (1,)), ((), ())), preferred_element_type=F32)


def rolled(values, shift):
    shift = shift % values.shape[1]
    return values if shift == 0 else pltpu.roll(values, shift, 1)


def border_selection_one():
    lane = iota((1, 128), 1)
    source = jnp.full((1, 128), -1, jnp.int32)
    source = jnp.where(lane == 0, 511, source)
    source = jnp.where((lane >= 1) & (lane <= 16), 32 * (lane - 1) + 31, source)
    source = jnp.where(lane == 17, 31, source)
    source = jnp.where((lane >= 32) & (lane < 64), 480 + lane - 32, source)
    source = jnp.where(lane == 64, 480, source)
    source = jnp.where((lane >= 65) & (lane <= 80), 32 * (lane - 65), source)
    source = jnp.where(lane == 81, 0, source)
    source = jnp.where(lane >= 96, lane - 96, source)
    return one_hot(512, source)


def column_placement_one():
    lane = iota((1, 1536), 1)
    offset = lane // 512
    y = lane % 512 // 32
    x = lane % 32
    source = jnp.where(x == 0, y + offset, jnp.where(x == 31, 64 + y + offset, -1))
    return one_hot(128, source)


def extension():
    lane = iota((1, 256), 1)
    y, x = lane // 20 - 2, lane % 20 - 2
    dy = jnp.where(y < 0, -1, jnp.where(y >= 8, 1, 0))
    dx = jnp.where(x < 0, -1, jnp.where(x >= 16, 1, 0))
    slot = 3 * (dy + 1) + dx + 1
    slot = jnp.where(slot == 4, 8, jnp.where(slot > 4, slot - 1, slot))
    source = 128 * slot + 16 * (y - 8 * dy) + x - 16 * dx
    return one_hot(1152, jnp.where(lane < 240, source, -1))


def interior_selection():
    lane = iota((1, 128), 1)
    return one_hot(256, 20 * (lane // 16 + 2) + lane % 16 + 2)


def pool_selection():
    lane = iota((1, 128), 1)
    return one_hot(512, 64 * (lane // 16) + 2 * (lane % 16))


def spread_selection():
    lane = iota((1, 512), 1)
    return one_hot(256, 20 * (lane // 64 + 2) + lane % 32 // 2 + 2)


def kernel(
    x_ref, w1_ref, w2_ref, cot_ref,
    out_ref, one_ref, two_ref,
    select_one, place_one, extend, pool_select, spread_select, interior_select,
    x_all, w1_cat, w2_own, w2_all, w2_cat, w2_turned,
    pack_one, recv_one, patches_one, hidden_one,
    p_own, p_recv, p_all, patches_two, c_recv, c_all, patches_d,
    g2_send, g2_pair, g2_part, g2_recv, g2_tiles, g2_far, g2_done,
    g1_send, g1_recv, g1_far, g1_done, both,
    z_sems, plane_sems, w2_sems, g2_sems, g1_sems,
):
    sx, sy, af = lax.axis_index("sx"), lax.axis_index("sy"), lax.axis_index("af")
    af_x, af_y = af % 4, af // 4
    core, half_y = sx % 2, sx // 2

    barrier = pltpu.get_barrier_semaphore()
    greeted = [
        {"sx": lax.rem(sx + dx, N_SX), "sy": lax.rem(sy + dy, N_SY)}
        for dx in (0, 1, N_SX - 1)
        for dy in (0, 1, N_SY - 1)
        if dx or dy
    ]
    greeted += [{"af": lax.rem(af + step, N_AF)} for step in (1, N_AF - 1)]
    greeted += [{"af": af_y * 4 + lax.rem(af_x + j, 4)} for j in (1, 2, 3)]
    greeted += [{"af": lax.rem(af_y + j, 4) * 4 + af_x} for j in (1, 2, 3)]
    greeted += [{"sy": lax.rem(sy + N_SY // 2, N_SY)}]
    for device in greeted:
        pl.semaphore_signal(barrier, inc=1, device_id=device, device_id_type=MESH)

    pl.semaphore_wait(barrier, len(greeted))

    pending = []

    class Group:
        def __init__(self, count, source, target, device, sems):
            self.count = count

            def copy(j):
                return pltpu.make_async_remote_copy(
                    src_ref=source(j),
                    dst_ref=target,
                    send_sem=sems.at[0, j],
                    recv_sem=sems.at[1, j],
                    device_id=device(j),
                    device_id_type=MESH,
                )

            self.copy = copy
            self.each(lambda copy: copy.start())
            pending.append(self.wait_send)

        def each(self, act):
            for j in range(1, self.count):
                act(self.copy(j))

        def wait_recv(self):
            self.each(lambda copy: copy.wait_recv())

        def wait_send(self):
            self.each(lambda copy: copy.wait_send())

    def ring(axis, me, count, source, target, sems):
        return Group(
            count,
            lambda j: source(lax.rem(me + j, count)),
            target.at[me],
            lambda j: {axis: lax.rem(me + j, count)},
            sems,
        )

    def exchange_planes(steps, target, sems):
        copies = []
        for way, (step, source, slot) in enumerate(steps):
            copy = pltpu.make_async_remote_copy(
                src_ref=source,
                dst_ref=target.at[slot],
                send_sem=sems.at[0, way],
                recv_sem=sems.at[1, way],
                device_id={"af": lax.rem(af + N_AF + step, N_AF)},
                device_id_type=MESH,
            )
            copy.start()
            pending.append(copy.wait_send)
            copies.append(copy)
        return copies

    def exchange_borders(source, target, sems):
        copies = []
        for slot, (dx, dy) in enumerate(SLOTS):
            copy = pltpu.make_async_remote_copy(
                src_ref=source,
                dst_ref=target.at[slot],
                send_sem=sems.at[0, slot],
                recv_sem=sems.at[1, slot],
                device_id={
                    "sx": lax.rem(sx + N_SX - dx, N_SX),
                    "sy": lax.rem(sy + N_SY - dy, N_SY),
                },
                device_id_type=MESH,
            )
            copy.start()
            pending.append(copy.wait_send)
            copies.append(copy)
        return copies

    def inside(dx, dy):
        good = True
        if dx:
            good = (sx > 0) if dx < 0 else (sx < N_SX - 1)
        if dy:
            row = (sy > 0) if dy < 0 else (sy < N_SY - 1)
            good = row if good is True else good & row
        return good

    def gather_columns(received, height, right):
        first = received[0].astype(F32)
        lane = iota(first.shape, 1)
        columns = jnp.zeros(first.shape, F32)
        for dx, start in ((-1, 0), (1, right)):
            for dy, cells in (
                (0, (lane >= start + 1) & (lane <= start + height)),
                (-1, lane == start),
                (1, lane == start + height + 1),
            ):
                values = received[SLOTS.index((dx, dy))].astype(F32)
                columns = jnp.where(cells & inside(dx, dy), values, columns)
        return columns.astype(BF16)

    def masked_rows(received, dy):
        values = received[SLOTS.index((0, dy))].astype(F32)
        return jnp.where(inside(0, dy), values, 0.0)

    def extended(received, own):
        planes = []
        for slot, (dx, dy) in enumerate(SLOTS):
            planes.append(jnp.where(inside(dx, dy), received[slot].astype(F32), 0.0).astype(BF16))
        joined = jnp.concatenate(planes + [own], axis=1)
        return dot(joined, extend[...]).astype(BF16)

    x_copies = exchange_planes(
        [(-1, x_ref.at[0], 3), (1, x_ref.at[1], 0)], x_all, z_sems.at[0]
    )
    for t in range(7):
        rows = []
        for half in range(2):
            pair = []
            for k in (14 * half + 2 * t, 14 * half + 2 * t + 1):
                pair.append(w2_ref[k].astype(F32) if k < 27 else jnp.zeros((8, 64), F32))
            rows.append(jnp.concatenate(pair, axis=1))
        w2_own[:, 128 * t : 128 * t + 128] = jnp.concatenate(rows, axis=0).astype(BF16)
    w2_far = Group(
        4,
        lambda j: w2_own,
        w2_all.at[af_x, af_y],
        lambda j: {"af": lax.rem(af_y + j, 4) * 4 + af_x},
        w2_sems.at[0],
    )
    c_copies = exchange_borders(cot_ref, c_recv, plane_sems.at[2])

    x_all[1] = x_ref[0]
    x_all[2] = x_ref[1]
    w2_all[af_x, af_y] = w2_own[...]
    select_one[...] = border_selection_one()
    place_one[...] = column_placement_one()
    w1_cat[...] = w1_ref[...].astype(F32).reshape(864, 64).T.astype(BF16)
    extend[...] = extension()
    pool_select[...] = pool_selection()
    spread_select[...] = spread_selection()
    interior_select[...] = interior_selection()
    patches_two[2880:2944] = jnp.zeros((64, 256), BF16)
    for copy in x_copies:
        copy.wait_recv()

    field = x_all[...].reshape(128, 512).astype(F32)
    row = iota((128, 512), 0)
    outer = ((row < 32) & (af == 0)) | ((row >= 96) & (af == N_AF - 1))
    field = jnp.where(outer, 0.0, field)
    pack_one[...] = dot(field.astype(BF16), select_one[...]).astype(BF16)
    copies = exchange_borders(pack_one, recv_one, plane_sems.at[0])
    w2_far.wait_recv()
    w2_near = Group(
        4,
        lambda j: w2_all.at[af_x],
        w2_all.at[af_x],
        lambda j: {"af": af_y * 4 + lax.rem(af_x + j, 4)},
        w2_sems.at[1],
    )
    for copy in c_copies:
        copy.wait_recv()
    c_all[1] = extended(c_recv, cot_ref[...])
    for copy in copies:
        copy.wait_recv()
    columns = dot(gather_columns(recv_one, 16, 64), place_one[...])
    above, below = masked_rows(recv_one, -1), masked_rows(recv_one, 1)
    lane = iota((128, 128), 1)
    x = iota((128, 512), 1) % 32
    for b in range(3):
        for c in range(3):
            dy, dx = b - 1, c - 1
            moved = rolled(field, -(32 * dy + dx))
            if dy == -1:
                first = jnp.where(lane < 32, rolled(above, -(32 + dx)), moved[:, :128])
                moved = jnp.concatenate([first, moved[:, 128:]], axis=1)
            if dy == 1:
                final = jnp.where(lane >= 96, rolled(below, -dx), moved[:, 384:])
                moved = jnp.concatenate([moved[:, :384], final], axis=1)
            if dx:
                placed = columns[:, 512 * b : 512 * b + 512]
                moved = jnp.where(x == (0 if dx < 0 else 31), placed, moved)
            moved = moved.astype(BF16)
            start = 32 * (3 * b + c)
            for z in range(4):
                patches_one[288 * z + start : 288 * z + start + 32] = moved[32 * z : 32 * z + 32]
    total = None
    for z in range(2):
        hidden = dot(w1_cat[...], patches_one[288 * z : 288 * z + 864])
        hidden_one[z] = hidden
        total = leaky(hidden) if total is None else total + leaky(hidden)
    total = total + rolled(total, -1)
    total = total + rolled(total, -32)
    p_own[...] = dot((total * 0.125).astype(BF16), pool_select[...]).astype(BF16)

    copies = exchange_borders(p_own, p_recv, plane_sems.at[1])
    c_steps = exchange_planes(
        [(-1, c_all.at[1], 2), (1, c_all.at[1], 0)], c_all, z_sems.at[2]
    )
    w2_near.wait_recv()
    pieces = [w2_all[p % 4, p // 4].astype(F32) for p in range(16)]
    for half in range(2):
        filters = jnp.concatenate([piece[8 * half : 8 * half + 8] for piece in pieces], axis=0)
        w2_cat[half] = filters.astype(BF16)
        turned = filters.T.astype(BF16)
        for place in range(14):
            k = 14 * half + place
            if k < 27:
                start = 128 * (26 - k)
                w2_turned[:, start : start + 128] = turned[64 * place : 64 * place + 64]
    for copy in copies:
        copy.wait_recv()
    p_all[2] = extended(p_recv, p_own[...])
    copies = exchange_planes(
        [(step, p_all.at[2], 2 - step) for step in (-2, -1, 1, 2)], p_all, z_sems.at[1]
    )

    def shift_plane(values, target, start, channels):
        for b in range(3):
            for c in range(3):
                moved = rolled(values, -(20 * (b - 1) + c - 1)).astype(BF16)
                place = start + channels * (3 * b + c)
                target[place : place + channels] = moved

    shift_plane(p_all[2].astype(F32), patches_two, 576 * 2, 64)
    for z, copy in ((4, copies[0]), (3, copies[1]), (1, copies[2]), (0, copies[3])):
        copy.wait_recv()
        values = p_all[z].astype(F32)
        exists = (af + z >= 2) & (af + z < N_AF + 2)
        shift_plane(jnp.where(exists, values, 0.0), patches_two, 576 * z, 64)
    for copy in c_steps:
        copy.wait_recv()

    lane = iota((128, 256), 1)
    y, x = lane // 20 - 2, lane % 20 - 2
    own = (y >= 0) & (y < 8) & (x >= 0) & (x < 16)
    grid_y, grid_x = 8 * sy + y, 16 * sx + x
    on_grid = (grid_y >= 0) & (grid_y < 8 * N_SY) & (grid_x >= 0) & (grid_x < 16 * N_SX)
    for z in range(3):
        start = 576 * z
        hidden = dot(w2_cat[0], patches_two[start : start + 896])
        hidden = hidden + dot(w2_cat[1], patches_two[start + 896 : start + 1792])
        if z == 1:
            out_ref[...] = dot(leaky(hidden).astype(BF16), interior_select[...]).astype(BF16)
        delta = (c_all[z].astype(F32) * slope(hidden)).astype(BF16).astype(F32)
        exists = (af + z >= 1) & (af + z < N_AF + 1)
        delta = jnp.where(on_grid & exists, delta, 0.0)
        if z == 1:
            delta_two = jnp.where(own, delta, 0.0).astype(BF16)
        shift_plane(delta, patches_d, 1152 * z, 128)

    pooled_grad = dot(w2_turned[...], patches_d[...]).astype(BF16)

    spread = dot(pooled_grad, spread_select[...]) * 0.125
    total = None
    for z in range(2):
        delta_one = (spread * slope(hidden_one[z])).T.astype(BF16)
        part = dot(patches_one[288 * z : 288 * z + 864], delta_one)
        total = part if total is None else total + part
    rest = jnp.concatenate([total[512:], jnp.zeros((160, 64), F32)], axis=0)
    sums = jnp.concatenate([total[:512], rest], axis=1).astype(BF16)
    g1_send[...] = sums.reshape(4, 4, 32, 128)

    def near(j):
        return lax.rem(sx + j // 4, N_SX), lax.rem(af_x + j % 4, 4)

    def near_device(j):
        return {"sx": near(j)[0], "af": af_y * 4 + near(j)[1]}

    def far_device(j):
        return {"af": lax.rem(af_y + j, 4) * 4 + af_x}

    g1_near = Group(16, lambda j: g1_send.at[near(j)], g1_recv.at[sx, af_x], near_device, g1_sems.at[0])
    g1_recv[sx, af_x] = g1_send[sx, af_x]

    halves = []
    for half in range(2):
        start = 576 + 896 * half
        part = dot_nt(delta_two, patches_two[start : start + 896]).reshape(16, 1, 8, 896)
        halves.append(part)
    parts = jnp.concatenate(halves, axis=1).reshape(16, 16, 896).astype(BF16)
    parts = jnp.concatenate([parts, jnp.zeros((16, 16, 128), BF16)], axis=2)
    for p in range(16):
        for q in range(4):
            g2_send[q % 2, q // 2, p % 4, p // 4] = parts[p][:, 256 * q : 256 * q + 256]
    g2_core = Group(
        2,
        lambda j: g2_send.at[1 - core],
        g2_pair,
        lambda j: {"sx": sx + 1 - 2 * core},
        g2_sems.at[0],
    )

    g2_core.wait_recv()
    mine = g2_send[core].astype(F32) + g2_pair[...].astype(F32)
    g2_part[...] = mine.astype(BF16)

    def beside(j):
        return lax.rem(half_y + j // 4, 2), lax.rem(af_x + j % 4, 4)

    g2_near = Group(
        8,
        lambda j: g2_part.at[beside(j)],
        g2_recv.at[half_y, af_x],
        lambda j: {"sx": beside(j)[0] * 2 + core, "af": af_y * 4 + beside(j)[1]},
        g2_sems.at[1],
    )
    g2_recv[half_y, af_x] = g2_part[half_y, af_x]

    g1_near.wait_recv()
    g1_far[af_y] = jnp.sum(g1_recv[...].astype(F32).reshape(16, 32, 128), axis=0).astype(BF16)
    g1_far_group = Group(4, lambda j: g1_far.at[af_y], g1_far.at[af_y], far_device, g1_sems.at[1])

    g2_near.wait_recv()
    sums = jnp.sum(g2_recv[...].astype(F32).reshape(8, 4, 16, 256), axis=0)
    g2_tiles[...] = sums.astype(BF16)
    g2_far_group = Group(
        4,
        lambda j: g2_tiles.at[lax.rem(af_y + j, 4)],
        g2_far.at[af_y],
        far_device,
        g2_sems.at[2],
    )
    g2_far[af_y] = g2_tiles[af_y]

    g1_far_group.wait_recv()
    both[sy, 0] = jnp.sum(g1_far[...].astype(F32), axis=0).astype(BF16)

    def along_sy(j):
        return {"sy": lax.rem(sy + j, N_SY)}

    g1_sy_group = Group(N_SY, lambda j: both.at[sy, 0], both.at[sy, 0], along_sy, g1_sems.at[3])
    g2_far_group.wait_recv()
    sums = jnp.sum(g2_far[...].astype(F32), axis=0).astype(BF16)
    both[sy, 1, :16] = sums[:, :128]
    both[sy, 1, 16:] = sums[:, 128:]
    g2_sy_group = Group(N_SY, lambda j: both.at[sy, 1], both.at[sy, 1], along_sy, g2_sems.at[4])
    g1_sy_group.wait_recv()
    sums = jnp.sum(both[:, 0].astype(F32), axis=0)
    g1_done[sx, af_x] = (sums * 524288.0**-0.5).astype(BF16)
    g1_done_group = Group(
        16,
        lambda j: g1_done.at[sx, af_x],
        g1_done.at[sx, af_x],
        near_device,
        g1_sems.at[2],
    )
    g2_sy_group.wait_recv()
    sums = jnp.sum(both[:, 1].astype(F32), axis=0)
    g2_done[sx] = (sums * (1.0 / 256.0)).astype(BF16)
    g2_done_ring = ring("sx", sx, N_SX, lambda peer: g2_done.at[sx], g2_done, g2_sems.at[3])
    g2_done_ring.wait_recv()
    two_ref[...] = g2_done[...]
    g1_done_group.wait_recv()
    one_ref[...] = g1_done[...].reshape(16, 32, 128)

    for wait in pending:
        wait()


def unpack(output, one, two, output_ref, grad_one_ref, grad_two_ref):
    output_ref[...] = output[...]
    for k in range(27):
        half = 64 * (k // 16)
        grad_one_ref[k] = one[k % 16].astype(F32)[:, half : half + 64]
        half, place = k // 14, k % 14
        tile = two[place // 4].astype(F32)
        row, column = 16 * (place % 4 // 2) + 8 * half, 64 * (place % 2)
        grad_two_ref[k] = tile[row : row + 8, column : column + 64]


def per_device(inputs, weight_one, weight_two, cotangent):
    x = inputs.reshape(32, 2, 512).transpose(1, 0, 2)
    cot = cotangent.reshape(128, 128)
    vmem = pl.BlockSpec(memory_space=pltpu.VMEM)
    output, one, two = pl.pallas_call(
        kernel,
        out_shape=(
            jax.ShapeDtypeStruct((128, 128), BF16),
            jax.ShapeDtypeStruct((16, 32, 128), BF16),
            jax.ShapeDtypeStruct((4, 32, 128), BF16),
        ),
        in_specs=[vmem] * 4,
        out_specs=(vmem, vmem, vmem),
        scratch_shapes=[
            pltpu.VMEM((512, 128), BF16),
            pltpu.VMEM((128, 1536), BF16),
            pltpu.VMEM((1152, 256), BF16),
            pltpu.VMEM((512, 128), BF16),
            pltpu.VMEM((256, 512), BF16),
            pltpu.VMEM((256, 128), BF16),
            pltpu.VMEM((4, 32, 512), BF16),
            pltpu.VMEM((64, 864), BF16),
            pltpu.VMEM((16, 896), BF16),
            pltpu.VMEM((4, 4, 16, 896), BF16),
            pltpu.VMEM((2, 128, 896), BF16),
            pltpu.VMEM((64, 3456), BF16),
            pltpu.VMEM((128, 128), BF16),
            pltpu.VMEM((8, 128, 128), BF16),
            pltpu.VMEM((1152, 512), BF16),
            pltpu.VMEM((2, 64, 512), F32),
            pltpu.VMEM((64, 128), BF16),
            pltpu.VMEM((8, 64, 128), BF16),
            pltpu.VMEM((5, 64, 256), BF16),
            pltpu.VMEM((2944, 256), BF16),
            pltpu.VMEM((8, 128, 128), BF16),
            pltpu.VMEM((3, 128, 256), BF16),
            pltpu.VMEM((3456, 256), BF16),
            pltpu.VMEM((2, 2, 4, 4, 16, 256), BF16),
            pltpu.VMEM((2, 4, 4, 16, 256), BF16),
            pltpu.VMEM((2, 4, 4, 16, 256), BF16),
            pltpu.VMEM((2, 4, 4, 16, 256), BF16),
            pltpu.VMEM((4, 16, 256), BF16),
            pltpu.VMEM((4, 16, 256), BF16),
            pltpu.VMEM((4, 32, 128), BF16),
            pltpu.VMEM((4, 4, 32, 128), BF16),
            pltpu.VMEM((4, 4, 32, 128), BF16),
            pltpu.VMEM((4, 32, 128), BF16),
            pltpu.VMEM((4, 4, 32, 128), BF16),
            pltpu.VMEM((8, 2, 32, 128), BF16),
            pltpu.SemaphoreType.DMA((3, 2, 4)),
            pltpu.SemaphoreType.DMA((3, 2, 8)),
            pltpu.SemaphoreType.DMA((2, 2, 4)),
            pltpu.SemaphoreType.DMA((5, 2, 8)),
            pltpu.SemaphoreType.DMA((4, 2, 16)),
        ],
        compiler_params=pltpu.CompilerParams(
            collective_id=0, has_side_effects=True, vmem_limit_bytes=48 * 2**20
        ),
    )(x, weight_one.transpose(0, 2, 1), weight_two, cot)
    output, grad_one, grad_two = pl.pallas_call(
        unpack,
        out_shape=(
            jax.ShapeDtypeStruct((128, 128), BF16),
            jax.ShapeDtypeStruct((27, 32, 64), F32),
            jax.ShapeDtypeStruct((27, 8, 64), F32),
        ),
        in_specs=[vmem] * 3,
        out_specs=(vmem, vmem, vmem),
        compiler_params=pltpu.CompilerParams(vmem_limit_bytes=16 * 2**20),
    )(output, one, two)
    return output.reshape(128, 1, 1, 1, 128), grad_one.transpose(0, 2, 1), grad_two


def solution(mesh):
    placed = (
        P(None, "af", "sy", "sx", None),
        P(),
        P(None, "af", None),
        P(None, "af", "sy", "sx", None),
    )
    return jax.shard_map(
        per_device,
        mesh=mesh,
        in_specs=placed,
        out_specs=(P(None, "af", "sy", "sx", None), P(), P(None, "af", None)),
        check_vma=False,
    )
```

```python
import functools

import jax
import jax.numpy as jnp
from jax import lax
from jax.experimental import pallas as pl
from jax.experimental.pallas import tpu as pltpu
from jax.sharding import PartitionSpec as P

MESH = pl.DeviceIdType.MESH
BF16 = jnp.bfloat16
F32 = jnp.float32
N_SX, N_SY, N_AF = 4, 8, 16
SLOTS = [(dx, dy) for dy in (-1, 0, 1) for dx in (-1, 0, 1) if (dx, dy) != (0, 0)]


def iota(shape, axis):
    return lax.broadcasted_iota(jnp.int32, shape, axis)


def leaky(values):
    return jnp.where(values > 0, values, 0.3 * values)


def slope(values):
    return jnp.where(values > 0, 1.0, 0.3)


def one_hot(rows, source):
    return (iota((rows, source.shape[1]), 0) == source).astype(F32).astype(BF16)


def dot(a, b):
    return jnp.dot(a, b, preferred_element_type=F32)


def dot_nt(a, b):
    return lax.dot_general(a, b, (((1,), (1,)), ((), ())), preferred_element_type=F32)


def rolled(values, shift):
    shift = shift % values.shape[1]
    return values if shift == 0 else pltpu.roll(values, shift, 1)


def border_selection_one():
    lane = iota((1, 128), 1)
    source = jnp.full((1, 128), -1, jnp.int32)
    source = jnp.where(lane == 0, 511, source)
    source = jnp.where((lane >= 1) & (lane <= 16), 32 * (lane - 1) + 31, source)
    source = jnp.where(lane == 17, 31, source)
    source = jnp.where((lane >= 32) & (lane < 64), 480 + lane - 32, source)
    source = jnp.where(lane == 64, 480, source)
    source = jnp.where((lane >= 65) & (lane <= 80), 32 * (lane - 65), source)
    source = jnp.where(lane == 81, 0, source)
    source = jnp.where(lane >= 96, lane - 96, source)
    return one_hot(512, source)


def column_placement_one():
    lane = iota((1, 1536), 1)
    offset = lane // 512
    y = lane % 512 // 32
    x = lane % 32
    source = jnp.where(x == 0, y + offset, jnp.where(x == 31, 64 + y + offset, -1))
    return one_hot(128, source)


def extension():
    lane = iota((1, 256), 1)
    y, x = lane // 20 - 2, lane % 20 - 2
    dy = jnp.where(y < 0, -1, jnp.where(y >= 8, 1, 0))
    dx = jnp.where(x < 0, -1, jnp.where(x >= 16, 1, 0))
    slot = 3 * (dy + 1) + dx + 1
    slot = jnp.where(slot == 4, 8, jnp.where(slot > 4, slot - 1, slot))
    source = 128 * slot + 16 * (y - 8 * dy) + x - 16 * dx
    return one_hot(1152, jnp.where(lane < 240, source, -1))


def interior_selection():
    lane = iota((1, 128), 1)
    return one_hot(256, 20 * (lane // 16 + 2) + lane % 16 + 2)


def pool_selection():
    lane = iota((1, 128), 1)
    return one_hot(512, 64 * (lane // 16) + 2 * (lane % 16))


def spread_selection():
    lane = iota((1, 512), 1)
    return one_hot(256, 20 * (lane // 64 + 2) + lane % 32 // 2 + 2)


def kernel(
    x_ref, w1_ref, w2_ref, cot_ref,
    out_ref, one_ref, two_ref,
    select_one, place_one, extend, pool_select, spread_select, interior_select,
    x_all, w1_cat, w2_own, w2_all, w2_cat, w2_turned,
    pack_one, recv_one, patches_one, hidden_one,
    p_own, p_recv, p_all, patches_two, c_recv, c_all, patches_d,
    g2_send, g2_pair, g2_part, g2_recv, g2_tiles, g2_far, g2_done,
    g1_send, g1_recv, g1_far, g1_done, both,
    z_sems, plane_sems, w2_sems, g2_sems, g1_sems,
):
    sx, sy, af = lax.axis_index("sx"), lax.axis_index("sy"), lax.axis_index("af")
    af_x, af_y = af % 4, af // 4
    core, half_y = sx % 2, sx // 2

    barrier = pltpu.get_barrier_semaphore()
    greeted = [
        {"sx": lax.rem(sx + dx, N_SX), "sy": lax.rem(sy + dy, N_SY)}
        for dx in (0, 1, N_SX - 1)
        for dy in (0, 1, N_SY - 1)
        if dx or dy
    ]
    greeted += [{"af": lax.rem(af + step, N_AF)} for step in (1, N_AF - 1)]
    greeted += [{"af": af_y * 4 + lax.rem(af_x + j, 4)} for j in (1, 3)]
    greeted += [{"af": lax.rem(af_y + j, 4) * 4 + af_x} for j in (1, 2, 3)]
    greeted += [{"sy": lax.rem(sy + N_SY // 2, N_SY)}]
    for device in greeted:
        pl.semaphore_signal(barrier, inc=1, device_id=device, device_id_type=MESH)

    pl.semaphore_wait(barrier, len(greeted))

    pending = []

    class Group:
        def __init__(self, count, source, target, device, sems):
            self.count = count

            def copy(j):
                return pltpu.make_async_remote_copy(
                    src_ref=source(j),
                    dst_ref=target,
                    send_sem=sems.at[0, j],
                    recv_sem=sems.at[1, j],
                    device_id=device(j),
                    device_id_type=MESH,
                )

            self.copy = copy
            self.each(lambda copy: copy.start())
            pending.append(self.wait_send)

        def each(self, act):
            for j in range(1, self.count):
                act(self.copy(j))

        def wait_recv(self):
            self.each(lambda copy: copy.wait_recv())

        def wait_send(self):
            self.each(lambda copy: copy.wait_send())

    def ring(axis, me, count, source, target, sems):
        return Group(
            count,
            lambda j: source(lax.rem(me + j, count)),
            target.at[me],
            lambda j: {axis: lax.rem(me + j, count)},
            sems,
        )

    def exchange_planes(steps, target, sems):
        copies = []
        for way, (step, source, slot) in enumerate(steps):
            copy = pltpu.make_async_remote_copy(
                src_ref=source,
                dst_ref=target.at[slot],
                send_sem=sems.at[0, way],
                recv_sem=sems.at[1, way],
                device_id={"af": lax.rem(af + N_AF + step, N_AF)},
                device_id_type=MESH,
            )
            copy.start()
            pending.append(copy.wait_send)
            copies.append(copy)
        return copies

    def exchange_borders(source, target, sems):
        copies = []
        for slot, (dx, dy) in enumerate(SLOTS):
            copy = pltpu.make_async_remote_copy(
                src_ref=source,
                dst_ref=target.at[slot],
                send_sem=sems.at[0, slot],
                recv_sem=sems.at[1, slot],
                device_id={
                    "sx": lax.rem(sx + N_SX - dx, N_SX),
                    "sy": lax.rem(sy + N_SY - dy, N_SY),
                },
                device_id_type=MESH,
            )
            copy.start()
            pending.append(copy.wait_send)
            copies.append(copy)
        return copies

    def inside(dx, dy):
        good = True
        if dx:
            good = (sx > 0) if dx < 0 else (sx < N_SX - 1)
        if dy:
            row = (sy > 0) if dy < 0 else (sy < N_SY - 1)
            good = row if good is True else good & row
        return good

    def gather_columns(received, height, right):
        first = received[0].astype(F32)
        lane = iota(first.shape, 1)
        columns = jnp.zeros(first.shape, F32)
        for dx, start in ((-1, 0), (1, right)):
            for dy, cells in (
                (0, (lane >= start + 1) & (lane <= start + height)),
                (-1, lane == start),
                (1, lane == start + height + 1),
            ):
                values = received[SLOTS.index((dx, dy))].astype(F32)
                columns = jnp.where(cells & inside(dx, dy), values, columns)
        return columns.astype(BF16)

    def masked_rows(received, dy):
        values = received[SLOTS.index((0, dy))].astype(F32)
        return jnp.where(inside(0, dy), values, 0.0)

    def extended(received, own):
        planes = []
        for slot, (dx, dy) in enumerate(SLOTS):
            planes.append(jnp.where(inside(dx, dy), received[slot].astype(F32), 0.0).astype(BF16))
        joined = jnp.concatenate(planes + [own], axis=1)
        return dot(joined, extend[...]).astype(BF16)

    x_copies = exchange_planes(
        [(-1, x_ref.at[0], 3), (1, x_ref.at[1], 0)], x_all, z_sems.at[0]
    )
    for t in range(7):
        rows = []
        for half in range(2):
            pair = []
            for k in (14 * half + 2 * t, 14 * half + 2 * t + 1):
                pair.append(w2_ref[k].astype(F32) if k < 27 else jnp.zeros((8, 64), F32))
            rows.append(jnp.concatenate(pair, axis=1))
        w2_own[:, 128 * t : 128 * t + 128] = jnp.concatenate(rows, axis=0).astype(BF16)
    w2_far = Group(
        4,
        lambda j: w2_own,
        w2_all.at[af_x, af_y],
        lambda j: {"af": lax.rem(af_y + j, 4) * 4 + af_x},
        w2_sems.at[0],
    )

    x_all[1] = x_ref[0]
    x_all[2] = x_ref[1]
    w2_all[af_x, af_y] = w2_own[...]
    select_one[...] = border_selection_one()
    place_one[...] = column_placement_one()
    w1_cat[...] = w1_ref[...].astype(F32).reshape(864, 64).T.astype(BF16)
    extend[...] = extension()
    pool_select[...] = pool_selection()
    spread_select[...] = spread_selection()
    interior_select[...] = interior_selection()
    patches_two[2880:2944] = jnp.zeros((64, 256), BF16)
    c_copies = exchange_borders(cot_ref, c_recv, plane_sems.at[2])
    for copy in x_copies:
        copy.wait_recv()

    field = x_all[...].reshape(128, 512).astype(F32)
    row = iota((128, 512), 0)
    outer = ((row < 32) & (af == 0)) | ((row >= 96) & (af == N_AF - 1))
    field = jnp.where(outer, 0.0, field)
    pack_one[...] = dot(field.astype(BF16), select_one[...]).astype(BF16)
    copies = exchange_borders(pack_one, recv_one, plane_sems.at[0])
    w2_far.wait_recv()
    w2_near = Group(
        4,
        lambda j: w2_all.at[af_x],
        w2_all.at[af_x],
        lambda j: {"af": af_y * 4 + lax.rem(af_x + j, 4)},
        w2_sems.at[1],
    )
    for copy in c_copies:
        copy.wait_recv()
    c_all[1] = extended(c_recv, cot_ref[...])
    for copy in copies:
        copy.wait_recv()
    columns = dot(gather_columns(recv_one, 16, 64), place_one[...])
    above, below = masked_rows(recv_one, -1), masked_rows(recv_one, 1)
    lane = iota((128, 128), 1)
    x = iota((128, 512), 1) % 32
    for b in range(3):
        for c in range(3):
            dy, dx = b - 1, c - 1
            moved = rolled(field, -(32 * dy + dx))
            if dy == -1:
                first = jnp.where(lane < 32, rolled(above, -(32 + dx)), moved[:, :128])
                moved = jnp.concatenate([first, moved[:, 128:]], axis=1)
            if dy == 1:
                final = jnp.where(lane >= 96, rolled(below, -dx), moved[:, 384:])
                moved = jnp.concatenate([moved[:, :384], final], axis=1)
            if dx:
                placed = columns[:, 512 * b : 512 * b + 512]
                moved = jnp.where(x == (0 if dx < 0 else 31), placed, moved)
            moved = moved.astype(BF16)
            start = 32 * (3 * b + c)
            for z in range(4):
                patches_one[288 * z + start : 288 * z + start + 32] = moved[32 * z : 32 * z + 32]
    total = None
    for z in range(2):
        hidden = dot(w1_cat[...], patches_one[288 * z : 288 * z + 864])
        hidden_one[z] = hidden
        total = leaky(hidden) if total is None else total + leaky(hidden)
    total = total + rolled(total, -1)
    total = total + rolled(total, -32)
    p_own[...] = dot((total * 0.125).astype(BF16), pool_select[...]).astype(BF16)

    copies = exchange_borders(p_own, p_recv, plane_sems.at[1])
    c_steps = exchange_planes(
        [(-1, c_all.at[1], 2), (1, c_all.at[1], 0)], c_all, z_sems.at[2]
    )
    w2_near.wait_recv()
    pieces = [w2_all[p % 4, p // 4].astype(F32) for p in range(16)]
    for half in range(2):
        filters = jnp.concatenate([piece[8 * half : 8 * half + 8] for piece in pieces], axis=0)
        w2_cat[half] = filters.astype(BF16)
        turned = filters.T.astype(BF16)
        for place in range(14):
            k = 14 * half + place
            if k < 27:
                start = 128 * (26 - k)
                w2_turned[:, start : start + 128] = turned[64 * place : 64 * place + 64]
    for copy in copies:
        copy.wait_recv()
    p_all[2] = extended(p_recv, p_own[...])
    copies = exchange_planes(
        [(step, p_all.at[2], 2 - step) for step in (-2, -1, 1, 2)], p_all, z_sems.at[1]
    )

    def shift_plane(values, target, start, channels):
        for b in range(3):
            for c in range(3):
                moved = rolled(values, -(20 * (b - 1) + c - 1)).astype(BF16)
                place = start + channels * (3 * b + c)
                target[place : place + channels] = moved

    shift_plane(p_all[2].astype(F32), patches_two, 576 * 2, 64)
    for z, copy in ((4, copies[0]), (3, copies[1]), (1, copies[2]), (0, copies[3])):
        copy.wait_recv()
        values = p_all[z].astype(F32)
        exists = (af + z >= 2) & (af + z < N_AF + 2)
        shift_plane(jnp.where(exists, values, 0.0), patches_two, 576 * z, 64)
    for copy in c_steps:
        copy.wait_recv()

    lane = iota((128, 256), 1)
    y, x = lane // 20 - 2, lane % 20 - 2
    own = (y >= 0) & (y < 8) & (x >= 0) & (x < 16)
    grid_y, grid_x = 8 * sy + y, 16 * sx + x
    on_grid = (grid_y >= 0) & (grid_y < 8 * N_SY) & (grid_x >= 0) & (grid_x < 16 * N_SX)
    for z in range(3):
        start = 576 * z
        hidden = dot(w2_cat[0], patches_two[start : start + 896])
        hidden = hidden + dot(w2_cat[1], patches_two[start + 896 : start + 1792])
        if z == 1:
            out_ref[...] = dot(leaky(hidden).astype(BF16), interior_select[...]).astype(BF16)
        delta = (c_all[z].astype(F32) * slope(hidden)).astype(BF16).astype(F32)
        exists = (af + z >= 1) & (af + z < N_AF + 1)
        delta = jnp.where(on_grid & exists, delta, 0.0)
        if z == 1:
            delta_two = jnp.where(own, delta, 0.0).astype(BF16)
        shift_plane(delta, patches_d, 1152 * z, 128)

    pooled_grad = dot(w2_turned[...], patches_d[...]).astype(BF16)

    spread = dot(pooled_grad, spread_select[...]) * 0.125
    total = None
    for z in range(2):
        delta_one = (spread * slope(hidden_one[z])).T.astype(BF16)
        part = dot(patches_one[288 * z : 288 * z + 864], delta_one)
        total = part if total is None else total + part
    rest = jnp.concatenate([total[512:], jnp.zeros((160, 64), F32)], axis=0)
    sums = jnp.concatenate([total[:512], rest], axis=1).astype(BF16)
    g1_send[...] = sums.reshape(4, 4, 32, 128)

    def near(j):
        return lax.rem(sx + j // 4, N_SX), lax.rem(af_x + j % 4, 4)

    def near_device(j):
        return {"sx": near(j)[0], "af": af_y * 4 + near(j)[1]}

    def far_device(j):
        return {"af": lax.rem(af_y + j, 4) * 4 + af_x}

    g1_near = Group(16, lambda j: g1_send.at[near(j)], g1_recv.at[sx, af_x], near_device, g1_sems.at[0])
    g1_recv[sx, af_x] = g1_send[sx, af_x]

    halves = []
    for half in range(2):
        start = 576 + 896 * half
        part = dot_nt(delta_two, patches_two[start : start + 896]).reshape(16, 1, 8, 896)
        halves.append(part)
    parts = jnp.concatenate(halves, axis=1).reshape(16, 16, 896).astype(BF16)
    parts = jnp.concatenate([parts, jnp.zeros((16, 16, 128), BF16)], axis=2)
    for p in range(16):
        for q in range(4):
            g2_send[q % 2, q // 2, p % 4, p // 4] = parts[p][:, 256 * q : 256 * q + 256]
    g2_core = Group(
        2,
        lambda j: g2_send.at[1 - core],
        g2_pair,
        lambda j: {"sx": sx + 1 - 2 * core},
        g2_sems.at[0],
    )

    g2_core.wait_recv()
    mine = g2_send[core].astype(F32) + g2_pair[...].astype(F32)
    g2_part[...] = mine.astype(BF16)

    def beside(j):
        return lax.rem(half_y + j // 4, 2), lax.rem(af_x + j % 4, 4)

    g2_near = Group(
        8,
        lambda j: g2_part.at[beside(j)],
        g2_recv.at[half_y, af_x],
        lambda j: {"sx": beside(j)[0] * 2 + core, "af": af_y * 4 + beside(j)[1]},
        g2_sems.at[1],
    )
    g2_recv[half_y, af_x] = g2_part[half_y, af_x]

    g1_near.wait_recv()
    g1_far[af_y] = jnp.sum(g1_recv[...].astype(F32).reshape(16, 32, 128), axis=0).astype(BF16)
    g1_far_group = Group(4, lambda j: g1_far.at[af_y], g1_far.at[af_y], far_device, g1_sems.at[1])

    g2_near.wait_recv()
    sums = jnp.sum(g2_recv[...].astype(F32).reshape(8, 4, 16, 256), axis=0)
    g2_tiles[...] = sums.astype(BF16)
    g2_far_group = Group(
        4,
        lambda j: g2_tiles.at[lax.rem(af_y + j, 4)],
        g2_far.at[af_y],
        far_device,
        g2_sems.at[2],
    )
    g2_far[af_y] = g2_tiles[af_y]

    g1_far_group.wait_recv()
    both[sy, 0] = jnp.sum(g1_far[...].astype(F32), axis=0).astype(BF16)

    def along_sy(j):
        return {"sy": lax.rem(sy + j, N_SY)}

    g1_sy_group = Group(N_SY, lambda j: both.at[sy, 0], both.at[sy, 0], along_sy, g1_sems.at[3])
    g2_far_group.wait_recv()
    sums = jnp.sum(g2_far[...].astype(F32), axis=0).astype(BF16)
    both[sy, 1, :16] = sums[:, :128]
    both[sy, 1, 16:] = sums[:, 128:]
    g2_sy_group = Group(N_SY, lambda j: both.at[sy, 1], both.at[sy, 1], along_sy, g2_sems.at[4])
    g1_sy_group.wait_recv()
    sums = jnp.sum(both[:, 0].astype(F32), axis=0)
    g1_done[sx, af_x] = (sums * 524288.0**-0.5).astype(BF16)
    g1_done_group = Group(
        16,
        lambda j: g1_done.at[sx, af_x],
        g1_done.at[sx, af_x],
        near_device,
        g1_sems.at[2],
    )
    g2_sy_group.wait_recv()
    sums = jnp.sum(both[:, 1].astype(F32), axis=0)
    g2_done[sx] = (sums * (1.0 / 256.0)).astype(BF16)
    g2_done_ring = ring("sx", sx, N_SX, lambda peer: g2_done.at[sx], g2_done, g2_sems.at[3])
    g2_done_ring.wait_recv()
    two_ref[...] = g2_done[...]
    g1_done_group.wait_recv()
    one_ref[...] = g1_done[...].reshape(16, 32, 128)

    for wait in pending:
        wait()


def unpack(output, one, two, output_ref, grad_one_ref, grad_two_ref):
    output_ref[...] = output[...]
    for k in range(27):
        half = 64 * (k // 16)
        grad_one_ref[k] = one[k % 16].astype(F32)[:, half : half + 64]
        half, place = k // 14, k % 14
        tile = two[place // 4].astype(F32)
        row, column = 16 * (place % 4 // 2) + 8 * half, 64 * (place % 2)
        grad_two_ref[k] = tile[row : row + 8, column : column + 64]


def per_device(inputs, weight_one, weight_two, cotangent):
    x = inputs.reshape(32, 2, 512).transpose(1, 0, 2)
    cot = cotangent.reshape(128, 128)
    vmem = pl.BlockSpec(memory_space=pltpu.VMEM)
    output, one, two = pl.pallas_call(
        kernel,
        out_shape=(
            jax.ShapeDtypeStruct((128, 128), BF16),
            jax.ShapeDtypeStruct((16, 32, 128), BF16),
            jax.ShapeDtypeStruct((4, 32, 128), BF16),
        ),
        in_specs=[vmem] * 4,
        out_specs=(vmem, vmem, vmem),
        scratch_shapes=[
            pltpu.VMEM((512, 128), BF16),
            pltpu.VMEM((128, 1536), BF16),
            pltpu.VMEM((1152, 256), BF16),
            pltpu.VMEM((512, 128), BF16),
            pltpu.VMEM((256, 512), BF16),
            pltpu.VMEM((256, 128), BF16),
            pltpu.VMEM((4, 32, 512), BF16),
            pltpu.VMEM((64, 864), BF16),
            pltpu.VMEM((16, 896), BF16),
            pltpu.VMEM((4, 4, 16, 896), BF16),
            pltpu.VMEM((2, 128, 896), BF16),
            pltpu.VMEM((64, 3456), BF16),
            pltpu.VMEM((128, 128), BF16),
            pltpu.VMEM((8, 128, 128), BF16),
            pltpu.VMEM((1152, 512), BF16),
            pltpu.VMEM((2, 64, 512), F32),
            pltpu.VMEM((64, 128), BF16),
            pltpu.VMEM((8, 64, 128), BF16),
            pltpu.VMEM((5, 64, 256), BF16),
            pltpu.VMEM((2944, 256), BF16),
            pltpu.VMEM((8, 128, 128), BF16),
            pltpu.VMEM((3, 128, 256), BF16),
            pltpu.VMEM((3456, 256), BF16),
            pltpu.VMEM((2, 2, 4, 4, 16, 256), BF16),
            pltpu.VMEM((2, 4, 4, 16, 256), BF16),
            pltpu.VMEM((2, 4, 4, 16, 256), BF16),
            pltpu.VMEM((2, 4, 4, 16, 256), BF16),
            pltpu.VMEM((4, 16, 256), BF16),
            pltpu.VMEM((4, 16, 256), BF16),
            pltpu.VMEM((4, 32, 128), BF16),
            pltpu.VMEM((4, 4, 32, 128), BF16),
            pltpu.VMEM((4, 4, 32, 128), BF16),
            pltpu.VMEM((4, 32, 128), BF16),
            pltpu.VMEM((4, 4, 32, 128), BF16),
            pltpu.VMEM((8, 2, 32, 128), BF16),
            pltpu.SemaphoreType.DMA((3, 2, 4)),
            pltpu.SemaphoreType.DMA((3, 2, 8)),
            pltpu.SemaphoreType.DMA((2, 2, 4)),
            pltpu.SemaphoreType.DMA((5, 2, 8)),
            pltpu.SemaphoreType.DMA((4, 2, 16)),
        ],
        compiler_params=pltpu.CompilerParams(
            collective_id=0, has_side_effects=True, vmem_limit_bytes=48 * 2**20
        ),
    )(x, weight_one.transpose(0, 2, 1), weight_two, cot)
    output, grad_one, grad_two = pl.pallas_call(
        unpack,
        out_shape=(
            jax.ShapeDtypeStruct((128, 128), BF16),
            jax.ShapeDtypeStruct((27, 32, 64), F32),
            jax.ShapeDtypeStruct((27, 8, 64), F32),
        ),
        in_specs=[vmem] * 3,
        out_specs=(vmem, vmem, vmem),
        compiler_params=pltpu.CompilerParams(vmem_limit_bytes=16 * 2**20),
    )(output, one, two)
    return output.reshape(128, 1, 1, 1, 128), grad_one.transpose(0, 2, 1), grad_two


def solution(mesh):
    placed = (
        P(None, "af", "sy", "sx", None),
        P(),
        P(None, "af", None),
        P(None, "af", "sy", "sx", None),
    )
    return jax.shard_map(
        per_device,
        mesh=mesh,
        in_specs=placed,
        out_specs=(P(None, "af", "sy", "sx", None), P(), P(None, "af", None)),
        check_vma=False,
    )
```
